256 devices in a mesh: grp: 16 (over y, x), blk: 16 (over z, core).
Axes of the slice: x: 4, y: 4, z: 8, core: 2. Of those that a mesh axis runs over, the one named last changes fastest.
Arguments:
- queries: bfloat16 [32768, 1024], P(('grp', 'blk')), may hold values from -8 to 8
- key_rows: bfloat16 [32768, 128], P(('grp', 'blk')), may hold values from -8 to 8
- values: bfloat16 [32768, 128], P(('grp', 'blk')), may hold values from -6 to 6
- out_grad: bfloat16 [32768, 1024], P(('grp', 'blk')), may hold values from -6 to 6
- span_order: int32 [16], replicated, may hold values from 0 to 15, each once
Outputs:
- attended: bfloat16 [32768, 1024], P(('grp', 'blk'))
- grad_queries: bfloat16 [32768, 1024], P(('grp', 'blk'))
- grad_keys: bfloat16 [32768, 128], P(('grp', 'blk'))
- grad_values: bfloat16 [32768, 128], P(('grp', 'blk'))
The draws below stay inside these ranges and needn't reach their ends.
Inputs may be any that keep to these rules, and one draw needn't show every extreme that they name: `span_order`: a permutation of 0 to 15.
All inputs are finite; a program needn't handle non-finite values.
Results may differ from the reference program's by a relative error of at most 0.015.
Values may be sent and summed in bfloat16 or wider, within the bound.
A program may use at most 64 MiB of HBM per device.

```python
import math
import jax
import jax.numpy as jnp
from jax import lax

GROUP = 8
HEAD = 128
ROWS = 128
TOKENS = 32768
N_GRP = 16
N_BLK = 16


def base_values(key, columns):
    return jnp.clip(jax.random.normal(key, (TOKENS, columns)), -4.0, 4.0)


def draw_queries(key, part):
    values_now = base_values(jax.random.fold_in(key, 11), GROUP * HEAD)
    return values_now.astype(jnp.bfloat16)


def draw_key_rows(key, part):
    values_now = base_values(jax.random.fold_in(key, 13), HEAD)
    return values_now.astype(jnp.bfloat16)


def levels(rng, extent, shards, smallest, top_value):
    def one(position, blocks):
        steps = jax.random.uniform(jax.random.fold_in(jax.random.fold_in(rng, 6), position), (blocks,), jnp.float32, smallest / len(shards), top_value / len(shards))
        return jnp.repeat(jnp.exp(steps), extent[position] // blocks).reshape((-1,) + (1,) * (len(extent) - position - 1))

    factor_of = one(*shards[0])
    for cut in shards[1:]:
        factor_of = factor_of * one(*cut)
    return factor_of


def bell_draw(stream_key, extent, scale, most, cuts=(), kind=jnp.bfloat16):
    result = scale * jax.random.normal(stream_key, extent, jnp.float32)
    if cuts:
        result = result * levels(stream_key, extent, cuts, -0.22, 0.18)
    return jnp.clip(result, -most, most).astype(kind)


def setup_inputs(seed: int = 0) -> dict:
    streams_of = jax.random.split(jax.random.key(seed), 6)
    return {
        "queries": draw_queries(jax.random.fold_in(streams_of[5], 71), 0),
        "key_rows": draw_key_rows(jax.random.fold_in(streams_of[5], 71), 0),
        "values": bell_draw(streams_of[2], (TOKENS, HEAD), 1.0, 6.0, ((0, 256),)),
        "out_grad": bell_draw(streams_of[3], (TOKENS, GROUP * HEAD), 1.0, 6.0, ((0, 256),)),
        "span_order": jax.random.permutation(streams_of[4], N_BLK).astype(jnp.int32),
    }


NEG_FILL = -1e+30

def rounded(matrix):
    return lax.optimization_barrier(matrix.astype(jnp.bfloat16)).astype(jnp.float32)

def token_positions(span_order):
    halfway = N_GRP // 2
    grp_ids = jnp.arange(N_GRP, dtype=jnp.int32)[:, None, None]
    lead_part = span_order.astype(jnp.int32)[None, :, None]
    section = jnp.where(grp_ids < halfway, lead_part, 2 * N_BLK - 1 - lead_part)
    inside = jnp.arange(ROWS, dtype=jnp.int32)[None, None, :]
    return section * (halfway * ROWS) + grp_ids % halfway * ROWS + inside

def block_pass(query_blk, grad_blk, query_pos, kv_rows, key_pos):
    factor = 1.0 / math.sqrt(HEAD)
    highest = lax.Precision.HIGHEST
    query_count = query_blk.shape[0]
    query_heads = query_blk.astype(jnp.float32).reshape(query_count, GROUP, HEAD)
    grad_heads = grad_blk.astype(jnp.float32).reshape(query_count, GROUP, HEAD)
    key_head = kv_rows[:, :HEAD].astype(jnp.float32)
    value_head = kv_rows[:, HEAD:].astype(jnp.float32)
    raw_scores = jnp.einsum('qhd,kd->hqk', query_heads, key_head, precision=highest) * factor
    visible = (key_pos[None, :] <= query_pos[:, None])[None, :, :]
    scores = jnp.where(visible, raw_scores, NEG_FILL)
    row_top = lax.optimization_barrier(jnp.max(scores, axis=2, keepdims=True))
    weights = jnp.where(visible, jnp.exp(scores - row_top), 0.0)
    row_total = lax.optimization_barrier(jnp.sum(weights, axis=2, keepdims=True))
    blended = jnp.einsum('hqk,kd->hqd', rounded(weights), value_head, precision=highest)
    out_heads = rounded(blended / row_total)
    row_delta = lax.optimization_barrier(jnp.sum(jnp.transpose(grad_heads, (1, 0, 2)) * out_heads, axis=2, keepdims=True))
    normed = weights / row_total
    value_grad = jnp.einsum('hqk,qhd->kd', rounded(normed), grad_heads, precision=highest)
    prob_grad = jnp.einsum('qhd,kd->hqk', grad_heads, value_head, precision=highest)
    score_grad = rounded(normed * (prob_grad - row_delta))
    query_grad = factor * jnp.einsum('hqk,kd->qhd', score_grad, key_head, precision=highest)
    key_grad = factor * jnp.einsum('hqk,qhd->kd', score_grad, query_heads, precision=highest)
    out_rows = jnp.transpose(out_heads, (1, 0, 2)).reshape(query_count, GROUP * HEAD).astype(jnp.bfloat16)
    query_rows = query_grad.reshape(query_count, GROUP * HEAD).astype(jnp.bfloat16)
    return (out_rows, query_rows, jnp.concatenate([key_grad, value_grad], axis=1))

def reference(queries, key_rows, values, out_grad, span_order):
    width = GROUP * HEAD
    places = token_positions(span_order)
    query_grid = queries.reshape(N_GRP, N_BLK, ROWS, width)
    grad_grid = out_grad.reshape(N_GRP, N_BLK, ROWS, width)
    pair_grid = jnp.concatenate([key_rows, values], axis=1).reshape(N_GRP, N_BLK, ROWS, 2 * HEAD)

    def column(grid, blk_id):
        picked = lax.dynamic_index_in_dim(grid, blk_id, 1, keepdims=False)
        return picked.reshape((N_GRP * ROWS,) + grid.shape[3:])

    def one_block(blk_id):
        nearby = [(blk_id + N_BLK - 1) % N_BLK, blk_id, (blk_id + 1) % N_BLK]
        kv_all = jnp.concatenate([column(pair_grid, neighbor) for neighbor in nearby], axis=0)
        key_pos = jnp.concatenate([column(places, neighbor) for neighbor in nearby], axis=0)
        out_rows, query_rows, kv_grad = block_pass(column(query_grid, blk_id), column(grad_grid, blk_id), column(places, blk_id), kv_all, key_pos)
        return (out_rows, query_rows, kv_grad.reshape(3, N_GRP * ROWS, 2 * HEAD))
    out_all, query_all, kv_parts = lax.map(one_block, jnp.arange(N_BLK, dtype=jnp.int32))
    kv_total = kv_parts[:, 1] + jnp.roll(kv_parts[:, 0], -1, axis=0) + jnp.roll(kv_parts[:, 2], 1, axis=0)

    def storage(stacked):
        breadth = stacked.shape[-1]
        return jnp.transpose(stacked.reshape(N_BLK, N_GRP, ROWS, breadth), (1, 0, 2, 3)).reshape(N_GRP * N_BLK * ROWS, breadth)
    kv_flat = storage(kv_total)
    return (storage(out_all), storage(query_all), kv_flat[:, :HEAD].astype(jnp.bfloat16), kv_flat[:, HEAD:].astype(jnp.bfloat16))
```

```python
import functools
import math

import jax
import jax.numpy as jnp
from jax import lax
from jax.experimental import pallas as pl
from jax.experimental.pallas import tpu as pltpu
from jax.sharding import PartitionSpec as P

HEAD = 128
ROWS = 128
WIDE = 512
NEG = -1e30
SCALE = 1.0 / math.sqrt(HEAD)
EXP2_SCALE = SCALE * math.log2(math.e)
F32 = jnp.float32
BF16 = jnp.bfloat16

AXIS_OF = (1, 0, 3, 2)


def dot(a, b):
    return jnp.dot(a, b, preferred_element_type=F32)


def kernel(
    q_ref, k_ref, v_ref, do_ref, order_ref,
    att_ref, gq_ref, gk_ref, gv_ref,
    k_own, v_own, k_far, v_far, k_sib, v_sib,
    q_in, do_in, q_t, q_n, do_t, do_n,
    s_far, s_sib, s_own, s_tri,
    w_far, w_sib, w_own, w_tri,
    top, total, out_t, dq_t, delta,
    acc_far, acc_own, g_sib, g_sib_in,
    red_out, red_in, far_out, far_in, o_out, dq_out,
    gat_send, gat_recv, sib_send, sib_recv, far_send, far_recv,
    tile_send, tile_recv, par_send, par_recv,
    gs_send, gs_recv, red_send, red_recv,
):
    grp = lax.axis_index("grp")
    blk = lax.axis_index("blk")
    y, x = lax.div(grp, 4), lax.rem(grp, 4)
    core = lax.rem(blk, 2)
    sib_blk = blk + 1 - 2 * core
    far_blk = lax.rem(blk + 15 + 2 * core, 16)
    side = lax.div(grp, 8)
    low = jnp.where(grp < 8, grp, 15 - grp)

    def flip(v):
        return v + 1 - 2 * lax.rem(v, 2)

    def near(grp_id):
        return {"grp": grp_id, "blk": blk}

    flips = (
        near(flip(y) * 4 + x),
        near((3 - y) * 4 + x),
        near(y * 4 + flip(x)),
        near(y * 4 + 3 - x),
    )
    partner = near(15 - grp)
    sibling = {"grp": grp, "blk": sib_blk}
    farther = {"grp": grp, "blk": far_blk}

    def place(grp_id):
        py, px = lax.div(grp_id, 4), lax.rem(grp_id, 4)
        return (
            lax.div(py, 2), lax.rem(lax.div(py + 1, 2), 2),
            lax.div(px, 2), lax.rem(lax.div(px + 1, 2), 2),
        )

    mine = place(grp)
    remote = functools.partial(
        pltpu.make_async_remote_copy, device_id_type=pl.DeviceIdType.MESH
    )

    def grid_slice(full, other=None):
        picks = []
        for axis in range(4):
            if axis in full:
                picks.append(pl.ds(0, 2))
            elif axis == other:
                picks.append(pl.ds(1 - mine[axis], 1))
            else:
                picks.append(pl.ds(mine[axis], 1))
        return tuple(picks)

    barrier = pltpu.get_barrier_semaphore()
    for dev in flips + (partner, sibling, farther):
        pl.semaphore_signal(barrier, inc=1, device_id=dev, device_id_type=pl.DeviceIdType.MESH)

    k_own[mine] = k_ref[...]
    v_own[mine] = v_ref[...]
    pl.semaphore_wait(barrier, 7)

    own_cols = pl.ds(pl.multiple_of(side * WIDE, WIDE), WIDE)
    other_cols = pl.ds(pl.multiple_of((1 - side) * WIDE, WIDE), WIDE)

    def gather_copy(quarter, step):
        ref = (k_own, v_own)[quarter // 2]
        rows = pl.ds(64 * (quarter % 2), 64)
        full = [AXIS_OF[(quarter + t) % 4] for t in range(step)]
        where = grid_slice(full) + (rows,)
        return remote(
            src_ref=ref.at[where], dst_ref=ref.at[where],
            send_sem=gat_send.at[quarter, step], recv_sem=gat_recv.at[quarter, step],
            device_id=flips[(quarter + step) % 4],
        )

    def pass_on(quarter, step, to_sib):
        own = (k_own, v_own)[quarter // 2]
        dest = ((k_sib, v_sib) if to_sib else (k_far, v_far))[quarter // 2]
        rows = pl.ds(64 * (quarter % 2), 64)
        full = [AXIS_OF[(quarter + t) % 4] for t in range(step)]
        where = grid_slice(full, AXIS_OF[(quarter + step) % 4]) + (rows,)
        sends, recvs = (sib_send, sib_recv) if to_sib else (far_send, far_recv)
        return remote(
            src_ref=own.at[where], dst_ref=dest.at[where],
            send_sem=sends.at[quarter, step], recv_sem=recvs.at[quarter, step],
            device_id=sibling if to_sib else farther,
        )

    def tile_copy(index):
        own = (k_own, v_own)[index // 2]
        dest = ((k_sib, v_sib), (k_far, v_far))[index % 2][index // 2]
        where = grid_slice(())
        return remote(
            src_ref=own.at[where], dst_ref=dest.at[where],
            send_sem=tile_send.at[index], recv_sem=tile_recv.at[index],
            device_id=(sibling, farther)[index % 2],
        )

    q_copy = remote(
        src_ref=q_ref.at[:, other_cols], dst_ref=q_in, send_sem=par_send.at[0],
        recv_sem=par_recv.at[0], device_id=partner,
    )
    do_copy = remote(
        src_ref=do_ref.at[:, other_cols], dst_ref=do_in, send_sem=par_send.at[1],
        recv_sem=par_recv.at[1], device_id=partner,
    )

    for quarter in range(4):
        gather_copy(quarter, 0).start()
    for index in range(4):
        tile_copy(index).start()
    q_copy.start()

    def spread(source, cols, index, flat, stacked):
        for head in range(4):
            part = source[:, pl.ds(pl.multiple_of(cols + head * HEAD, HEAD), HEAD)]
            flat[index, :, pl.ds(head * HEAD, HEAD)] = part.T
            if stacked is not None:
                stacked[index, pl.ds(head * HEAD, HEAD), :] = part

    spread(q_ref, side * WIDE, side, q_t, q_n)

    for step in range(4):
        for quarter in range(4):
            gather_copy(quarter, step).wait_recv()
            if step < 3:
                gather_copy(quarter, step + 1).start()
            pass_on(quarter, step, True).start()
            pass_on(quarter, step, False).start()
        if step == 0:
            spread(do_ref, side * WIDE, side, do_t, None)
        if step == 1:
            do_copy.start()
        if step == 2:
            q_copy.wait_recv()
            spread(q_in, 0, 1 - side, q_t, q_n)

    my_rank = order_ref[blk]
    sib_pick = jnp.where(order_ref[sib_blk] < my_rank, 0, 1)
    far_pick = jnp.where(order_ref[far_blk] < my_rank, 0, 1)

    def tiles(ref, half, i):
        return ref[half, lax.div(i, 2), lax.rem(i, 2)].reshape(2 * ROWS, HEAD)

    def fold_max(s):
        return jnp.max(s.reshape(-1, 8, WIDE), axis=0)

    def fold_sum(s):
        return jnp.sum(s.reshape(-1, 8, WIDE), axis=0)

    def tri_unit(u):
        first = u <= low
        which = jnp.where(first, 0, 1)
        tile = jnp.where(first, u, u + 7 - low)
        return which, place(tile), (u == low) | (u == 8)

    top[...] = jnp.full((2, 8, WIDE), NEG, F32)

    def own_scores(i, _):
        s = dot(tiles(k_own, 0, i), q_t[1])
        s_own[i] = s
        top[1] = jnp.maximum(top[1], fold_max(s))
        return 0

    def tri_scores(u, _):
        which, tile, diag = tri_unit(u)
        s = dot(k_own[tile], q_t[which])
        key_row = lax.broadcasted_iota(jnp.int32, (ROWS, WIDE), 0)
        query_row = lax.rem(lax.broadcasted_iota(jnp.int32, (ROWS, WIDE), 1), ROWS)
        limit = query_row + jnp.where(diag, 0, ROWS)
        s = jnp.where(key_row <= limit, s, NEG)
        s_tri[u] = s
        top[which] = jnp.maximum(top[which], fold_max(s))
        return 0

    def side_scores(keys, scores, pick):
        def step(i, _):
            s = dot(tiles(keys, 0, i), q_t[1])
            scores[0, i] = s
            top_up = jnp.maximum(top[1], fold_max(s))
            t = dot(tiles(keys, pick, i), q_t[pick])
            scores[1, i] = t
            peak = fold_max(t)
            top[0] = jnp.maximum(top[0], jnp.where(pick == 0, peak, NEG))
            top[1] = jnp.maximum(top_up, jnp.where(pick == 1, peak, NEG))
            return 0

        lax.fori_loop(0, 4, step, 0)

    lax.fori_loop(0, 4, own_scores, 0)
    lax.fori_loop(0, 9, tri_scores, 0)

    def wait_tiles(to_sib):
        for index in (0, 2) if to_sib else (1, 3):
            tile_copy(index).wait_recv()
        for step in range(4):
            for quarter in range(4):
                pass_on(quarter, step, to_sib).wait_recv()

    do_copy.wait_recv()
    spread(do_in, 0, 1 - side, do_t, None)
    wait_tiles(True)
    side_scores(k_sib, s_sib, sib_pick)
    wait_tiles(False)
    side_scores(k_far, s_far, far_pick)

    for s in range(2):
        top[s, pl.ds(0, 1)] = jnp.max(top[s], axis=0, keepdims=True) * EXP2_SCALE
    total[...] = jnp.zeros((2, 8, WIDE), F32)
    out_t[...] = jnp.zeros((2, HEAD, WIDE), F32)

    def weigh(s, peak):
        w = jnp.exp2(s * EXP2_SCALE - peak)
        return w.astype(BF16), fold_sum(w)

    def own_weights(i, _):
        w, add = weigh(s_own[i], top[1, pl.ds(0, 1)])
        w_own[i] = w
        total[1] += add
        out_t[1] += dot(tiles(v_own, 0, i).T, w)
        return 0

    def tri_weights(u, _):
        which, tile, _ = tri_unit(u)
        w, add = weigh(s_tri[u], top[which, pl.ds(0, 1)])
        w_tri[u] = w
        total[which] += add
        out_t[which] += dot(v_own[tile].T, w)
        return 0

    def side_weights(vals, scores, weights, pick):
        def step(i, _):
            w, add = weigh(scores[0, i], top[1, pl.ds(0, 1)])
            weights[0, i] = w
            part = dot(tiles(vals, 0, i).T, w)
            w2, add2 = weigh(scores[1, i], top[pick, pl.ds(0, 1)])
            weights[1, i] = w2
            part2 = dot(tiles(vals, pick, i).T, w2)
            total[0] += jnp.where(pick == 0, add2, 0.0)
            total[1] += add + jnp.where(pick == 1, add2, 0.0)
            out_t[0] += jnp.where(pick == 0, part2, 0.0)
            out_t[1] += part + jnp.where(pick == 1, part2, 0.0)
            return 0

        lax.fori_loop(0, 4, step, 0)

    lax.fori_loop(0, 4, own_weights, 0)
    lax.fori_loop(0, 9, tri_weights, 0)
    side_weights(v_sib, s_sib, w_sib, sib_pick)
    side_weights(v_far, s_far, w_far, far_pick)

    o_copy = remote(
        src_ref=o_out, dst_ref=att_ref.at[:, own_cols], send_sem=par_send.at[2],
        recv_sem=par_recv.at[2], device_id=partner,
    )
    dq_copy = remote(
        src_ref=dq_out, dst_ref=gq_ref.at[:, own_cols], send_sem=par_send.at[3],
        recv_sem=par_recv.at[3], device_id=partner,
    )

    def finish(index, dest, base):
        recip = 1.0 / jnp.sum(total[index], axis=0, keepdims=True)
        o = (out_t[index] * recip).astype(BF16)
        grads = do_t[index].astype(F32)
        delta[index] = jnp.sum(grads * o.astype(F32), axis=0, keepdims=True) * recip
        scaled = (grads * recip).astype(BF16)
        do_t[index] = scaled
        for head in range(4):
            cols = slice(head * HEAD, (head + 1) * HEAD)
            do_n[index, cols, :] = scaled[:, cols].T
            dest[:, pl.ds(pl.multiple_of(base + head * HEAD, HEAD), HEAD)] = o[:, cols].T

    finish(1 - side, o_out, 0)
    o_copy.start()
    finish(side, att_ref, side * WIDE)

    dq_t[...] = jnp.zeros((2, HEAD, WIDE), F32)

    def back(keys, vals, w, index):
        dp = dot(vals, do_t[index])
        ds = (w.astype(F32) * (dp - delta[index])).astype(BF16)
        dv = dot(w, do_n[index])
        dk = dot(ds, q_n[index]) * SCALE
        return dk, dv, dot(keys.T, ds)

    def reduce_part(acc, quarter, step, send):
        full = [AXIS_OF[(quarter + t) % 4] for t in range(step + 1, 4)]
        where = grid_slice(full, AXIS_OF[(quarter + step) % 4] if send else None)
        return (quarter // 2,) + where + (pl.ds(64 * (quarter % 2), 64),)

    OFFSET = (0, 8, 12, 14)

    def reduce_copy(which, quarter, step):
        span = pl.ds(OFFSET[step], 8 >> step)
        return remote(
            src_ref=red_out.at[which, quarter, span], dst_ref=red_in.at[which, quarter, span],
            send_sem=red_send.at[which, quarter, step], recv_sem=red_recv.at[which, quarter, step],
            device_id=flips[(quarter + step) % 4],
        )

    def reduce_send(which, acc, step):
        for quarter in range(4):
            part = acc[reduce_part(acc, quarter, step, True)]
            red_out[which, quarter, pl.ds(OFFSET[step], 8 >> step)] = part.reshape(
                8 >> step, 64, HEAD
            ).astype(BF16)
            reduce_copy(which, quarter, step).start()

    def reduce_take(which, acc, step):
        for quarter in range(4):
            reduce_copy(which, quarter, step).wait_recv()
            where = reduce_part(acc, quarter, step, False)
            part = acc[where]
            came = red_in[which, quarter, pl.ds(OFFSET[step], 8 >> step)]
            acc[where] = part + came.astype(F32).reshape(part.shape)

    def side_back(keys, vals, weights, pick, store):
        def step(i, _):
            dk, dv, dq = back(tiles(keys, 0, i), tiles(vals, 0, i), weights[0, i], 1)
            dk2, dv2, dq2 = back(tiles(keys, pick, i), tiles(vals, pick, i), weights[1, i], pick)
            dq_t[0] += jnp.where(pick == 0, dq2, 0.0)
            dq_t[1] += dq + jnp.where(pick == 1, dq2, 0.0)
            store(i, 0, 0, dk + jnp.where(pick == 0, dk2, 0.0))
            store(i, 1, 0, dv + jnp.where(pick == 0, dv2, 0.0))
            store(i, 0, 1, jnp.where(pick == 1, dk2, 0.0))
            store(i, 1, 1, jnp.where(pick == 1, dv2, 0.0))
            return 0

        lax.fori_loop(0, 4, step, 0)

    def far_store(i, kind, half, value):
        acc_far[kind, half, lax.div(i, 2), lax.rem(i, 2)] = value.reshape(2, ROWS, HEAD)

    def sib_copy(i, kind, half):
        where = (kind, half, lax.div(i, 2), lax.rem(i, 2))
        sem = (i * 2 + kind) * 2 + half
        return remote(
            src_ref=g_sib.at[where], dst_ref=g_sib_in.at[where],
            send_sem=gs_send.at[sem], recv_sem=gs_recv.at[sem], device_id=sibling,
        )

    def sib_store(i, kind, half, value):
        g_sib[kind, half, lax.div(i, 2), lax.rem(i, 2)] = value.reshape(2, ROWS, HEAD).astype(BF16)
        sib_copy(i, kind, half).start()

    side_back(k_far, v_far, w_far, far_pick, far_store)
    reduce_send(0, acc_far, 0)
    side_back(k_sib, v_sib, w_sib, sib_pick, sib_store)
    reduce_take(0, acc_far, 0)
    reduce_send(0, acc_far, 1)

    def own_back(i, _):
        dk, dv, dq = back(tiles(k_own, 0, i), tiles(v_own, 0, i), w_own[i], 1)
        where = (lax.div(i, 2), lax.rem(i, 2))
        acc_own[(0, 0) + where] = dk.reshape(2, ROWS, HEAD)
        acc_own[(1, 0) + where] = dv.reshape(2, ROWS, HEAD)
        dq_t[1] += dq
        return 0

    lax.fori_loop(0, 4, own_back, 0)
    acc_own[:, 1] = jnp.zeros((2, 2, 2, 2, ROWS, HEAD), F32)
    reduce_take(0, acc_far, 1)
    reduce_send(0, acc_far, 2)

    def tri_back(u, _):
        which, tile, _ = tri_unit(u)
        dk, dv, dq = back(k_own[tile], v_own[tile], w_tri[u], which)
        acc_own[(0,) + tile] += dk
        acc_own[(1,) + tile] += dv
        dq_t[which] += dq
        return 0

    lax.fori_loop(0, 9, tri_back, 0)

    reduce_take(0, acc_far, 2)
    reduce_send(0, acc_far, 3)

    def add_sib(i, _):
        for kind in range(2):
            for half in range(2):
                sib_copy(i, kind, half).wait_recv()
                where = (kind, half, lax.div(i, 2), lax.rem(i, 2))
                acc_own[where] += g_sib_in[where].astype(F32)
        return 0

    lax.fori_loop(0, 4, add_sib, 0)
    reduce_send(1, acc_own, 0)

    def finish_dq(index, dest, base):
        grads = (dq_t[index] * SCALE).astype(BF16)
        for head in range(4):
            cols = slice(head * HEAD, (head + 1) * HEAD)
            dest[:, pl.ds(pl.multiple_of(base + head * HEAD, HEAD), HEAD)] = grads[:, cols].T

    finish_dq(1 - side, dq_out, 0)
    dq_copy.start()
    reduce_take(0, acc_far, 3)
    for kind in range(2):
        far_out[kind] = acc_far[(kind,) + mine].astype(BF16)
    far_copy = remote(
        src_ref=far_out, dst_ref=far_in, send_sem=par_send.at[4],
        recv_sem=par_recv.at[4], device_id=farther,
    )
    far_copy.start()
    finish_dq(side, gq_ref, side * WIDE)

    reduce_take(1, acc_own, 0)
    for step in range(1, 4):
        reduce_send(1, acc_own, step)
        reduce_take(1, acc_own, step)
    far_copy.wait_recv()
    gk_ref[...] = (acc_own[(0,) + mine] + far_in[0].astype(F32)).astype(BF16)
    gv_ref[...] = (acc_own[(1,) + mine] + far_in[1].astype(F32)).astype(BF16)

    o_copy.wait_recv()
    dq_copy.wait_recv()
    for copy in (q_copy, do_copy, o_copy, dq_copy, far_copy):
        copy.wait_send()
    for index in range(4):
        tile_copy(index).wait_send()
    for step in range(4):
        for quarter in range(4):
            gather_copy(quarter, step).wait_send()
            pass_on(quarter, step, True).wait_send()
            pass_on(quarter, step, False).wait_send()
            reduce_copy(0, quarter, step).wait_send()
            reduce_copy(1, quarter, step).wait_send()

    def drain_sib(i, _):
        for kind in range(2):
            for half in range(2):
                sib_copy(i, kind, half).wait_send()
        return 0

    lax.fori_loop(0, 4, drain_sib, 0)


def body(queries, key_rows, values, out_grad, span_order):
    vmem = pl.BlockSpec(memory_space=pltpu.VMEM)
    kv = pltpu.VMEM((2, 2, 2, 2, ROWS, HEAD), BF16)
    dma = pltpu.SemaphoreType.DMA
    return pl.pallas_call(
        kernel,
        out_shape=(
            jax.ShapeDtypeStruct(queries.shape, BF16),
            jax.ShapeDtypeStruct(queries.shape, BF16),
            jax.ShapeDtypeStruct(key_rows.shape, BF16),
            jax.ShapeDtypeStruct(key_rows.shape, BF16),
        ),
        in_specs=[vmem] * 4 + [pl.BlockSpec(memory_space=pltpu.SMEM)],
        out_specs=(vmem,) * 4,
        scratch_shapes=[
            kv, kv, kv, kv, kv, kv,
            pltpu.VMEM((ROWS, WIDE), BF16), pltpu.VMEM((ROWS, WIDE), BF16),
            pltpu.VMEM((2, HEAD, WIDE), BF16), pltpu.VMEM((2, WIDE, HEAD), BF16),
            pltpu.VMEM((2, HEAD, WIDE), BF16), pltpu.VMEM((2, WIDE, HEAD), BF16),
            pltpu.VMEM((2, 4, 256, WIDE), F32), pltpu.VMEM((2, 4, 256, WIDE), F32),
            pltpu.VMEM((4, 256, WIDE), F32), pltpu.VMEM((9, ROWS, WIDE), F32),
            pltpu.VMEM((2, 4, 256, WIDE), BF16), pltpu.VMEM((2, 4, 256, WIDE), BF16),
            pltpu.VMEM((4, 256, WIDE), BF16), pltpu.VMEM((9, ROWS, WIDE), BF16),
            pltpu.VMEM((2, 8, WIDE), F32), pltpu.VMEM((2, 8, WIDE), F32),
            pltpu.VMEM((2, HEAD, WIDE), F32), pltpu.VMEM((2, HEAD, WIDE), F32),
            pltpu.VMEM((2, 1, WIDE), F32),
            pltpu.VMEM((2, 2, 2, 2, 2, ROWS, HEAD), F32),
            pltpu.VMEM((2, 2, 2, 2, 2, ROWS, HEAD), F32),
            pltpu.VMEM((2, 2, 2, 2, 2, ROWS, HEAD), BF16),
            pltpu.VMEM((2, 2, 2, 2, 2, ROWS, HEAD), BF16),
            pltpu.VMEM((2, 4, 15, 64, HEAD), BF16), pltpu.VMEM((2, 4, 15, 64, HEAD), BF16),
            pltpu.VMEM((2, ROWS, HEAD), BF16), pltpu.VMEM((2, ROWS, HEAD), BF16),
            pltpu.VMEM((ROWS, WIDE), BF16), pltpu.VMEM((ROWS, WIDE), BF16),
            dma((4, 4)), dma((4, 4)), dma((4, 4)), dma((4, 4)), dma((4, 4)), dma((4, 4)),
            dma((4,)), dma((4,)), dma((5,)), dma((5,)),
            dma((16,)), dma((16,)), dma((2, 4, 4)), dma((2, 4, 4)),
        ],
        compiler_params=pltpu.CompilerParams(
            collective_id=0, has_side_effects=True, vmem_limit_bytes=56 * 1024 * 1024
        ),
        cost_estimate=pl.CostEstimate(
            flops=5 * 10**9, bytes_accessed=2 * 10**6, transcendentals=3 * 10**6
        ),
    )(queries, key_rows, values, out_grad, span_order)


def solution(mesh):
    rows = P(("grp", "blk"), None)
    return jax.shard_map(
        body,
        mesh=mesh,
        in_specs=(rows, rows, rows, rows, P()),
        out_specs=(rows, rows, rows, rows),
        check_vma=False,
    )
```

```python
import functools
import math

import jax
import jax.numpy as jnp
from jax import lax
from jax.experimental import pallas as pl
from jax.experimental.pallas import tpu as pltpu
from jax.sharding import PartitionSpec as P

HEAD = 128
ROWS = 128
WIDE = 512
NEG = -1e30
SCALE = 1.0 / math.sqrt(HEAD)
EXP2_SCALE = SCALE * math.log2(math.e)
F32 = jnp.float32
BF16 = jnp.bfloat16

WALK = (3, 0, 1, 2)
OFFSET = (0, 8, 12, 14)
FAR_V, OWN_V, FAR_K, OWN_K = range(4)
IS_OWN = (False, True, False, True)
KIND = (1, 1, 0, 0)


def dot(a, b):
    return jnp.dot(a, b, preferred_element_type=F32)


def dot_t(a, b):
    return lax.dot_general(a, b, (((1,), (1,)), ((), ())), preferred_element_type=F32)


def kernel(
    q_ref, k_ref, v_ref, do_ref, order_ref,
    att_ref, gq_ref, gk_ref, gv_ref,
    k_own, v_own, k_far, v_far, k_sib, v_sib,
    q_n, do_n,
    s_far, s_sib, s_own, w_far, w_sib, w_own,
    top, total, out_t, dq_t, delta,
    acc_far, acc_own, g_sib, g_sib_in,
    red_out, red_in, far_out, far_in, o_out, dq_out,
    gat_send, gat_recv, sib_send, sib_recv, far_send, far_recv,
    par_send, par_recv, gs_send, gs_recv, red_send, red_recv,
):
    grp = lax.axis_index("grp")
    blk = lax.axis_index("blk")
    y, x = lax.div(grp, 4), lax.rem(grp, 4)
    core = lax.rem(blk, 2)
    sib_blk = blk + 1 - 2 * core
    far_blk = lax.rem(blk + 15 + 2 * core, 16)
    side = lax.div(grp, 8)
    early_y = jnp.where(y < 2, y, 3 - y)
    span_tile = (early_y * 4 + x, (1 - early_y) * 4 + x)

    def flip(v):
        return v + 1 - 2 * lax.rem(v, 2)

    def near(grp_id):
        return {"grp": grp_id, "blk": blk}

    across = ((3 - y) * 4 + x, flip(y) * 4 + x, y * 4 + 3 - x, y * 4 + flip(x))
    partner = near(across[0])
    sibling = {"grp": grp, "blk": sib_blk}
    farther = {"grp": grp, "blk": far_blk}

    def place(grp_id):
        py, px = lax.div(grp_id, 4), lax.rem(grp_id, 4)
        return (
            lax.div(py, 2), lax.rem(lax.div(py + 1, 2), 2),
            lax.div(px, 2), lax.rem(lax.div(px + 1, 2), 2),
        )

    mine = place(grp)
    remote = functools.partial(
        pltpu.make_async_remote_copy, device_id_type=pl.DeviceIdType.MESH
    )

    barrier = pltpu.get_barrier_semaphore()
    for dev in tuple(near(a) for a in across) + (sibling, farther):
        pl.semaphore_signal(barrier, inc=1, device_id=dev, device_id_type=pl.DeviceIdType.MESH)

    k_own[mine] = k_ref[...]
    v_own[mine] = v_ref[...]
    own_cols = pl.ds(pl.multiple_of(side * WIDE, WIDE), WIDE)

    def stack(source, dest):
        for head in range(4):
            cols = pl.ds(pl.multiple_of(side * WIDE + head * HEAD, HEAD), HEAD)
            dest[side, pl.ds(head * HEAD, HEAD), :] = source[:, cols]

    pl.semaphore_wait(barrier, 6)

    def tile_at(mask):
        spot = []
        for axis in range(4):
            first = WALK.index(axis)
            on = (mask >> first) & 1
            on_back = (mask >> (3 - first)) & 1
            bit = mine[axis]
            if on == on_back:
                spot.append(1 - bit if on else bit)
            else:
                f = core if on_back else 1 - core
                spot.append(bit + f - 2 * bit * f)
        return tuple(spot)

    def toward(position):
        ahead, back = across[WALK[position]], across[WALK[3 - position]]
        return near(ahead + core * (back - ahead))

    own_kv, far_kv, sib_kv = (k_own, v_own), (k_far, v_far), (k_sib, v_sib)

    def hop(kind, mask, position, arriving):
        spot = tile_at(mask | (1 << position) if arriving else mask)
        return remote(
            src_ref=own_kv[kind].at[spot], dst_ref=own_kv[kind].at[spot],
            send_sem=gat_send.at[kind, position],
            recv_sem=gat_recv.at[kind, mask | (1 << position)],
            device_id=toward(position),
        )

    def hand_far(kind, mask):
        spot = tile_at(mask)
        return remote(
            src_ref=own_kv[kind].at[spot], dst_ref=far_kv[kind].at[spot],
            send_sem=far_send.at[kind], recv_sem=far_recv.at[kind], device_id=farther,
        )

    def far_all(kind):
        return remote(
            src_ref=own_kv[kind], dst_ref=far_kv[kind],
            send_sem=far_send.at[kind], recv_sem=far_recv.at[kind], device_id=farther,
        )

    def sib_all(kind):
        return remote(
            src_ref=own_kv[kind], dst_ref=sib_kv[kind],
            send_sem=sib_send.at[kind], recv_sem=sib_recv.at[kind], device_id=sibling,
        )

    def give_head(index, head):
        source, dest = ((q_ref, q_n), (do_ref, do_n))[index]
        cols = pl.ds(pl.multiple_of((1 - side) * WIDE + head * HEAD, HEAD), HEAD)
        return remote(
            src_ref=source.at[:, cols], dst_ref=dest.at[side, pl.ds(head * HEAD, HEAD)],
            send_sem=par_send.at[index], recv_sem=par_recv.at[index], device_id=partner,
        )

    def heads_all(index):
        dest = (q_n, do_n)[index].at[1 - side]
        return remote(
            src_ref=dest, dst_ref=dest,
            send_sem=par_send.at[index], recv_sem=par_recv.at[index], device_id=partner,
        )

    def relay(kind, mask):
        for position in range(mask.bit_length(), 4):
            hop(kind, mask, position, False).start()

    relay(0, 0)
    hand_far(0, 0).start()
    for head in range(4):
        give_head(0, head).start()
    relay(1, 0)
    stack(q_ref, q_n)
    stack(do_ref, do_n)
    late = [0]
    for level in range(1, 5):
        masks = [m for m in range(16) if bin(m).count("1") == level]
        for kind in range(2):
            for mask in masks:
                position = mask.bit_length() - 1
                hop(kind, mask - (1 << position), position, True).wait_recv()
                relay(kind, mask)
                if kind == 0:
                    hand_far(0, mask).start()
            if kind == 0:
                for mask in late:
                    hand_far(1, mask).start()
                if level == 4:
                    sib_all(0).start()
        late = masks
        if level == 3:
            for head in range(4):
                give_head(1, head).start()
    for mask in late:
        hand_far(1, mask).start()
    sib_all(1).start()

    my_rank = order_ref[blk]
    sib_pick = jnp.where(order_ref[sib_blk] < my_rank, 0, 1)
    far_pick = jnp.where(order_ref[far_blk] < my_rank, 0, 1)

    def half_of(ref, half):
        return ref[half].reshape(8 * ROWS, HEAD)

    def fold_max(s):
        return jnp.max(s.reshape(-1, 8, WIDE), axis=0)

    def fold_sum(s):
        return jnp.sum(s.reshape(-1, 8, WIDE), axis=0)

    def masked(s, half):
        row = lax.broadcasted_iota(jnp.int32, (ROWS, WIDE), 0)
        query = lax.rem(lax.broadcasted_iota(jnp.int32, (ROWS, WIDE), 1), ROWS)
        parts = []
        for tile in range(8):
            tile_y, tile_x = tile // 4, (0, 1, 3, 2)[tile % 4]
            rank = (1 - tile_y if half else tile_y) * 4 + tile_x
            seen = row <= query + (span_tile[half] - rank) * ROWS
            parts.append(jnp.where(seen, s[tile * ROWS : (tile + 1) * ROWS], NEG))
        return jnp.concatenate(parts, axis=0)

    top[...] = jnp.full((2, 8, WIDE), NEG, F32)

    def own_scores(job, half, which, mask):
        s = dot_t(half_of(k_own, half), q_n[which])
        if mask:
            s = masked(s, half)
        s_own[job] = s
        top[which] = jnp.maximum(top[which], fold_max(s))

    def side_scores(keys, scores, pick):
        s = dot_t(half_of(keys, 0), q_n[1])
        scores[0] = s
        top_up = jnp.maximum(top[1], fold_max(s))
        t = dot_t(half_of(keys, pick), q_n[pick])
        scores[1] = t
        peak = fold_max(t)
        top[0] = jnp.maximum(top[0], jnp.where(pick == 0, peak, NEG))
        top[1] = jnp.maximum(top_up, jnp.where(pick == 1, peak, NEG))

    heads_all(0).wait_recv()
    own_scores(0, 0, 1, False)
    own_scores(1, 0, 0, True)
    own_scores(2, 1, 1, True)
    sib_all(0).wait_recv()
    side_scores(k_sib, s_sib, sib_pick)
    far_all(0).wait_recv()
    side_scores(k_far, s_far, far_pick)

    for s in range(2):
        top[s, pl.ds(0, 1)] = jnp.max(top[s], axis=0, keepdims=True) * EXP2_SCALE
    total[...] = jnp.zeros((2, 8, WIDE), F32)
    out_t[...] = jnp.zeros((2, HEAD, WIDE), F32)

    def weigh(scores, weights, job, vals, half, which):
        peak = top[which, pl.ds(0, 1)]
        add = jnp.zeros((8, WIDE), F32)
        for i in range(4):
            rows = pl.ds(256 * i, 256)
            w = jnp.exp2(scores[job, rows] * EXP2_SCALE - peak)
            weights[job, rows] = w.astype(BF16)
            add = add + fold_sum(w)
        return add, dot(half_of(vals, half).T, weights[job])

    def own_weights(job, half, which):
        add, part = weigh(s_own, w_own, job, v_own, half, which)
        total[which] += add
        out_t[which] += part

    def side_weights(vals, scores, weights, pick):
        add, part = weigh(scores, weights, 0, vals, 0, 1)
        add2, part2 = weigh(scores, weights, 1, vals, pick, pick)
        total[0] += jnp.where(pick == 0, add2, 0.0)
        total[1] += add + jnp.where(pick == 1, add2, 0.0)
        out_t[0] += jnp.where(pick == 0, part2, 0.0)
        out_t[1] += part + jnp.where(pick == 1, part2, 0.0)

    own_weights(0, 0, 1)
    own_weights(1, 0, 0)
    own_weights(2, 1, 1)
    sib_all(1).wait_recv()
    side_weights(v_sib, s_sib, w_sib, sib_pick)
    far_all(1).wait_recv()
    side_weights(v_far, s_far, w_far, far_pick)

    o_copy = remote(
        src_ref=o_out, dst_ref=att_ref.at[:, own_cols], send_sem=par_send.at[2],
        recv_sem=par_recv.at[2], device_id=partner,
    )
    dq_copy = remote(
        src_ref=dq_out, dst_ref=gq_ref.at[:, own_cols], send_sem=par_send.at[3],
        recv_sem=par_recv.at[3], device_id=partner,
    )

    def finish(index, dest, base):
        recip = 1.0 / jnp.sum(total[index], axis=0, keepdims=True)
        for head in range(4):
            cols = slice(head * HEAD, (head + 1) * HEAD)
            recip_row = recip[:, cols]
            o = (out_t[index, :, pl.ds(head * HEAD, HEAD)] * recip_row).astype(BF16).T
            dest[:, pl.ds(pl.multiple_of(base + head * HEAD, HEAD), HEAD)] = o
            rows = pl.ds(head * HEAD, HEAD)
            grads = do_n[index, rows, :].astype(F32)
            along = jnp.sum(grads * o.astype(F32), axis=1, keepdims=True)
            along_row = jnp.broadcast_to(along, (ROWS, 8)).T[0:1]
            delta[index, :, pl.ds(head * HEAD, HEAD)] = along_row * recip_row
            recip_col = jnp.broadcast_to(recip_row, (8, ROWS)).T[:, 0:1]
            do_n[index, rows, :] = (grads * recip_col).astype(BF16)

    heads_all(1).wait_recv()
    finish(1 - side, o_out, 0)
    finish(side, att_ref, side * WIDE)

    def grid_slice(full, other=None):
        picks = []
        for axis in range(4):
            if axis in full:
                picks.append(pl.ds(0, 2))
            elif axis == other:
                picks.append(pl.ds(1 - mine[axis], 1))
            else:
                picks.append(pl.ds(mine[axis], 1))
        return tuple(picks)

    def reduce_part(family, quarter, step, send):
        full = [(quarter + t) % 4 for t in range(step + 1, 4)]
        where = grid_slice(full, (quarter + step) % 4 if send else None)
        return (KIND[family],) + where + (pl.ds(32 * quarter, 32),)

    def reduce_copy(family, quarter, step):
        span = pl.ds(OFFSET[step], 8 >> step)
        return remote(
            src_ref=red_out.at[family, quarter, span], dst_ref=red_in.at[family, quarter, span],
            send_sem=red_send.at[family, quarter, step],
            recv_sem=red_recv.at[family, quarter, step],
            device_id=near(across[(quarter + step) % 4]),
        )

    def held(family, where, step):
        part = (acc_own if IS_OWN[family] else acc_far)[where]
        if IS_OWN[family] and step == 0:
            part = part + g_sib_in[where].astype(F32)
        return part

    def reduce_send(family, step):
        for quarter in range(4):
            part = held(family, reduce_part(family, quarter, step, True), step)
            red_out[family, quarter, pl.ds(OFFSET[step], 8 >> step)] = part.reshape(
                8 >> step, 32, HEAD
            ).astype(BF16)
            reduce_copy(family, quarter, step).start()

    def reduce_take(family, step):
        acc = acc_own if IS_OWN[family] else acc_far
        for quarter in range(4):
            reduce_copy(family, quarter, step).wait_recv()
            where = reduce_part(family, quarter, step, False)
            part = held(family, where, step)
            came = red_in[family, quarter, pl.ds(OFFSET[step], 8 >> step)]
            acc[where] = part + came.astype(F32).reshape(part.shape)

    def reduce_next(family, step):
        reduce_take(family, step)
        reduce_send(family, step + 1)

    def far_copy(kind):
        return remote(
            src_ref=far_out.at[kind], dst_ref=far_in.at[kind], send_sem=par_send.at[4 + kind],
            recv_sem=par_recv.at[4 + kind], device_id=farther,
        )

    def far_finish(family):
        reduce_take(family, 3)
        kind = KIND[family]
        far_out[kind] = acc_far[(kind,) + mine].astype(BF16)
        far_copy(kind).start()

    def sib_copy(kind):
        return remote(
            src_ref=g_sib.at[kind], dst_ref=g_sib_in.at[kind],
            send_sem=gs_send.at[kind], recv_sem=gs_recv.at[kind], device_id=sibling,
        )

    def store(ref, kind, half, value):
        ref[kind, half] = value.reshape(2, 2, 2, ROWS, HEAD).astype(ref.dtype)

    def side_dv(weights, pick, ref):
        dv = dot(weights[0], do_n[1])
        dv2 = dot(weights[1], do_n[pick])
        store(ref, 1, 0, dv + jnp.where(pick == 0, dv2, 0.0))
        store(ref, 1, 1, jnp.where(pick == 1, dv2, 0.0))

    side_dv(w_far, far_pick, acc_far)
    reduce_send(FAR_V, 0)
    side_dv(w_sib, sib_pick, g_sib)
    sib_copy(1).start()
    o_copy.start()
    store(acc_own, 1, 0, dot(w_own[0], do_n[1]) + dot(w_own[1], do_n[0]))
    store(acc_own, 1, 1, dot(w_own[2], do_n[1]))
    sib_copy(1).wait_recv()
    reduce_send(OWN_V, 0)

    def back_dk(vals, half, weights, job, which):
        dp = dot_t(half_of(vals, half), do_n[which])
        ds = (weights[job].astype(F32) * (dp - delta[which])).astype(BF16)
        weights[job] = ds
        return dot(ds, q_n[which]) * SCALE

    def side_dk(vals, weights, pick, ref):
        dk = back_dk(vals, 0, weights, 0, 1)
        dk2 = back_dk(vals, pick, weights, 1, pick)
        store(ref, 0, 0, dk + jnp.where(pick == 0, dk2, 0.0))
        store(ref, 0, 1, jnp.where(pick == 1, dk2, 0.0))

    side_dk(v_far, w_far, far_pick, acc_far)
    reduce_next(FAR_V, 0)
    reduce_send(FAR_K, 0)
    side_dk(v_sib, w_sib, sib_pick, g_sib)
    sib_copy(0).start()
    reduce_next(OWN_V, 0)
    reduce_next(FAR_V, 1)
    store(acc_own, 0, 0, back_dk(v_own, 0, w_own, 0, 1) + back_dk(v_own, 0, w_own, 1, 0))
    reduce_next(FAR_K, 0)
    store(acc_own, 0, 1, back_dk(v_own, 1, w_own, 2, 1))
    sib_copy(0).wait_recv()
    reduce_send(OWN_K, 0)
    reduce_next(OWN_V, 1)
    reduce_next(FAR_V, 2)

    dq_t[...] = jnp.zeros((2, HEAD, WIDE), F32)

    def back_dq(keys, half, weights, job):
        return dot(half_of(keys, half).T, weights[job])

    def side_dq(keys, weights, pick):
        dq = back_dq(keys, 0, weights, 0)
        dq2 = back_dq(keys, pick, weights, 1)
        dq_t[0] += jnp.where(pick == 0, dq2, 0.0)
        dq_t[1] += dq + jnp.where(pick == 1, dq2, 0.0)

    side_dq(k_far, w_far, far_pick)
    reduce_next(FAR_K, 1)
    side_dq(k_sib, w_sib, sib_pick)
    reduce_next(OWN_K, 0)
    reduce_next(OWN_V, 2)
    far_finish(FAR_V)
    dq_t[0] += back_dq(k_own, 0, w_own, 1)
    dq_t[1] += back_dq(k_own, 0, w_own, 0) + back_dq(k_own, 1, w_own, 2)

    def finish_dq(index, dest, base):
        grads = (dq_t[index] * SCALE).astype(BF16)
        for head in range(4):
            cols = slice(head * HEAD, (head + 1) * HEAD)
            dest[:, pl.ds(pl.multiple_of(base + head * HEAD, HEAD), HEAD)] = grads[:, cols].T

    reduce_next(FAR_K, 2)
    finish_dq(1 - side, dq_out, 0)
    dq_copy.start()
    reduce_next(OWN_K, 1)
    finish_dq(side, gq_ref, side * WIDE)
    reduce_take(OWN_V, 3)
    far_finish(FAR_K)
    reduce_next(OWN_K, 2)
    far_copy(1).wait_recv()
    gv_ref[...] = (acc_own[(1,) + mine] + far_in[1].astype(F32)).astype(BF16)
    reduce_take(OWN_K, 3)
    far_copy(0).wait_recv()
    gk_ref[...] = (acc_own[(0,) + mine] + far_in[0].astype(F32)).astype(BF16)

    o_copy.wait_recv()
    dq_copy.wait_recv()
    for copy in (heads_all(0), heads_all(1), o_copy, dq_copy):
        copy.wait_send()
    for kind in range(2):
        far_copy(kind).wait_send()
        sib_copy(kind).wait_send()
        sib_all(kind).wait_send()
        far_all(kind).wait_send()
        for position in range(4):
            spans = tuple(
                pl.ds(0, 2 if axis >= 4 - position else 1) for axis in range(4)
            )
            part = own_kv[kind].at[spans]
            remote(
                src_ref=part, dst_ref=part, send_sem=gat_send.at[kind, position],
                recv_sem=gat_recv.at[kind, 0], device_id=toward(position),
            ).wait_send()
    for family in range(4):
        for step in range(4):
            for quarter in range(4):
                reduce_copy(family, quarter, step).wait_send()


def body(queries, key_rows, values, out_grad, span_order):
    vmem = pl.BlockSpec(memory_space=pltpu.VMEM)
    kv = pltpu.VMEM((2, 2, 2, 2, ROWS, HEAD), BF16)
    dma = pltpu.SemaphoreType.DMA
    return pl.pallas_call(
        kernel,
        out_shape=(
            jax.ShapeDtypeStruct(queries.shape, BF16),
            jax.ShapeDtypeStruct(queries.shape, BF16),
            jax.ShapeDtypeStruct(key_rows.shape, BF16),
            jax.ShapeDtypeStruct(key_rows.shape, BF16),
        ),
        in_specs=[vmem] * 4 + [pl.BlockSpec(memory_space=pltpu.SMEM)],
        out_specs=(vmem,) * 4,
        scratch_shapes=[
            kv, kv, kv, kv, kv, kv,
            pltpu.VMEM((2, WIDE, HEAD), BF16), pltpu.VMEM((2, WIDE, HEAD), BF16),
            pltpu.VMEM((2, 1024, WIDE), F32), pltpu.VMEM((2, 1024, WIDE), F32),
            pltpu.VMEM((3, 1024, WIDE), F32),
            pltpu.VMEM((2, 1024, WIDE), BF16), pltpu.VMEM((2, 1024, WIDE), BF16),
            pltpu.VMEM((3, 1024, WIDE), BF16),
            pltpu.VMEM((2, 8, WIDE), F32), pltpu.VMEM((2, 8, WIDE), F32),
            pltpu.VMEM((2, HEAD, WIDE), F32), pltpu.VMEM((2, HEAD, WIDE), F32),
            pltpu.VMEM((2, 1, WIDE), F32),
            pltpu.VMEM((2, 2, 2, 2, 2, ROWS, HEAD), F32),
            pltpu.VMEM((2, 2, 2, 2, 2, ROWS, HEAD), F32),
            pltpu.VMEM((2, 2, 2, 2, 2, ROWS, HEAD), BF16),
            pltpu.VMEM((2, 2, 2, 2, 2, ROWS, HEAD), BF16),
            pltpu.VMEM((4, 4, 15, 32, HEAD), BF16), pltpu.VMEM((4, 4, 15, 32, HEAD), BF16),
            pltpu.VMEM((2, ROWS, HEAD), BF16), pltpu.VMEM((2, ROWS, HEAD), BF16),
            pltpu.VMEM((ROWS, WIDE), BF16), pltpu.VMEM((ROWS, WIDE), BF16),
            dma((2, 4)), dma((2, 16)), dma((2,)), dma((2,)), dma((2,)), dma((2,)),
            dma((6,)), dma((6,)), dma((2,)), dma((2,)), dma((4, 4, 4)), dma((4, 4, 4)),
        ],
        compiler_params=pltpu.CompilerParams(
            collective_id=0, has_side_effects=True, vmem_limit_bytes=56 * 1024 * 1024
        ),
        cost_estimate=pl.CostEstimate(
            flops=5 * 10**9, bytes_accessed=2 * 10**6, transcendentals=3 * 10**6
        ),
    )(queries, key_rows, values, out_grad, span_order)


def solution(mesh):
    rows = P(("grp", "blk"), None)
    return jax.shard_map(
        body,
        mesh=mesh,
        in_specs=(rows, rows, rows, rows, P()),
        out_specs=(rows, rows, rows, rows),
        check_vma=False,
    )
```

```python
import functools
import math

import jax
import jax.numpy as jnp
from jax import lax
from jax.experimental import pallas as pl
from jax.experimental.pallas import tpu as pltpu
from jax.sharding import PartitionSpec as P

HEAD = 128
ROWS = 128
WIDE = 512
NEG = -1e30
SCALE = 1.0 / math.sqrt(HEAD)
EXP2_SCALE = SCALE * math.log2(math.e)
F32 = jnp.float32
BF16 = jnp.bfloat16

STEPS = (1, 3, 2)
OFFSET = (0, 8, 12, 14)
FAR_V, OWN_V, FAR_K, OWN_K = range(4)
IS_OWN = (False, True, False, True)
KIND = (1, 1, 0, 0)


def dot(a, b):
    return jnp.dot(a, b, preferred_element_type=F32)


def dot_t(a, b):
    return lax.dot_general(a, b, (((1,), (1,)), ((), ())), preferred_element_type=F32)


def kernel(
    q_ref, k_ref, v_ref, do_ref, order_ref,
    att_ref, gq_ref, gk_ref, gv_ref,
    k_own, v_own, k_far, v_far, k_sib, v_sib,
    q_n, do_n,
    s_far, s_sib, s_own, w_far, w_sib, w_own,
    top, total, out_t, dq_t, delta,
    acc_far, acc_own, g_sib, g_sib_in,
    red_out, red_in, far_out, far_in, o_out, dq_out,
    gat_send, gat_recv, sib_send, sib_recv, far_send, far_recv,
    par_send, par_recv, gs_send, gs_recv, red_send, red_recv,
):
    grp = lax.axis_index("grp")
    blk = lax.axis_index("blk")
    y, x = lax.div(grp, 4), lax.rem(grp, 4)
    core = lax.rem(blk, 2)
    sib_blk = blk + 1 - 2 * core
    far_blk = lax.rem(blk + 15 + 2 * core, 16)
    side = lax.div(grp, 8)
    early_y = jnp.where(y < 2, y, 3 - y)
    span_tile = (early_y * 4 + x, (1 - early_y) * 4 + x)

    def flip(v):
        return v + 1 - 2 * lax.rem(v, 2)

    def near(grp_id):
        return {"grp": grp_id, "blk": blk}

    def shifted(first, second):
        step_x = first + core * (second - first)
        step_y = second + core * (first - second)
        return lax.rem(y + step_y, 4) * 4 + lax.rem(x + step_x, 4)

    across = ((3 - y) * 4 + x, flip(y) * 4 + x, y * 4 + 3 - x, y * 4 + flip(x))
    partner = near(across[0])
    sibling = {"grp": grp, "blk": sib_blk}
    farther = {"grp": grp, "blk": far_blk}

    def place(grp_id):
        py, px = lax.div(grp_id, 4), lax.rem(grp_id, 4)
        return (
            lax.div(py, 2), lax.rem(lax.div(py + 1, 2), 2),
            lax.div(px, 2), lax.rem(lax.div(px + 1, 2), 2),
        )

    mine = place(grp)
    remote = functools.partial(
        pltpu.make_async_remote_copy, device_id_type=pl.DeviceIdType.MESH
    )

    barrier = pltpu.get_barrier_semaphore()
    meet = tuple(near(shifted(s, 0)) for s in STEPS) + tuple(near(shifted(0, s)) for s in STEPS)
    for dev in meet + (sibling, farther):
        pl.semaphore_signal(barrier, inc=1, device_id=dev, device_id_type=pl.DeviceIdType.MESH)

    k_own[mine] = k_ref[...]
    v_own[mine] = v_ref[...]
    own_cols = pl.ds(pl.multiple_of(side * WIDE, WIDE), WIDE)

    def stack(source, dest):
        for head in range(4):
            cols = pl.ds(pl.multiple_of(side * WIDE + head * HEAD, HEAD), HEAD)
            dest[side, pl.ds(head * HEAD, HEAD), :] = source[:, cols]

    pl.semaphore_wait(barrier, 8)

    own_kv, far_kv, sib_kv = (k_own, v_own), (k_far, v_far), (k_sib, v_sib)

    def spread(kind, first, second, arriving):
        along_first = second == 0
        if arriving:
            spot = place(shifted((4 - first) % 4, (4 - second) % 4))
        else:
            spot = mine if along_first else place(shifted((4 - first) % 4, 0))
        return remote(
            src_ref=own_kv[kind].at[spot], dst_ref=own_kv[kind].at[spot],
            send_sem=gat_send.at[kind, first * 4 + second],
            recv_sem=gat_recv.at[kind, first * 4 + second],
            device_id=near(shifted(first, 0) if along_first else shifted(0, second)),
        )

    def hand_far(kind, spot):
        return remote(
            src_ref=own_kv[kind].at[spot], dst_ref=far_kv[kind].at[spot],
            send_sem=far_send.at[kind], recv_sem=far_recv.at[kind], device_id=farther,
        )

    def far_all(kind):
        return remote(
            src_ref=own_kv[kind], dst_ref=far_kv[kind],
            send_sem=far_send.at[kind], recv_sem=far_recv.at[kind], device_id=farther,
        )

    def sib_all(kind):
        return remote(
            src_ref=own_kv[kind], dst_ref=sib_kv[kind],
            send_sem=sib_send.at[kind], recv_sem=sib_recv.at[kind], device_id=sibling,
        )

    def give_head(index, head):
        source, dest = ((q_ref, q_n), (do_ref, do_n))[index]
        cols = pl.ds(pl.multiple_of((1 - side) * WIDE + head * HEAD, HEAD), HEAD)
        return remote(
            src_ref=source.at[:, cols], dst_ref=dest.at[side, pl.ds(head * HEAD, HEAD)],
            send_sem=par_send.at[index], recv_sem=par_recv.at[index], device_id=partner,
        )

    def heads_all(index):
        dest = (q_n, do_n)[index].at[1 - side]
        return remote(
            src_ref=dest, dst_ref=dest,
            send_sem=par_send.at[index], recv_sem=par_recv.at[index], device_id=partner,
        )

    def begin(kind):
        for step in reversed(STEPS):
            spread(kind, step, 0, False).start()
        for step in reversed(STEPS):
            spread(kind, 0, step, False).start()

    def arrive(kind, first, second):
        spread(kind, first, second, True).wait_recv()
        if second == 0:
            for step in reversed(STEPS):
                spread(kind, first, step, False).start()
        hand_far(kind, place(shifted((4 - first) % 4, (4 - second) % 4))).start()

    begin(0)
    hand_far(0, mine).start()
    for head in range(4):
        give_head(0, head).start()
    begin(1)
    stack(q_ref, q_n)
    stack(do_ref, do_n)
    for step in STEPS:
        arrive(0, step, 0)
    for step in STEPS:
        arrive(0, 0, step)
    hand_far(1, mine).start()
    for step in STEPS:
        arrive(1, step, 0)
    for second in STEPS:
        for first in STEPS:
            arrive(0, first, second)
    sib_all(0).start()
    for head in range(4):
        give_head(1, head).start()

    my_rank = order_ref[blk]
    sib_pick = jnp.where(order_ref[sib_blk] < my_rank, 0, 1)
    far_pick = jnp.where(order_ref[far_blk] < my_rank, 0, 1)

    def half_of(ref, half):
        return ref[half].reshape(8 * ROWS, HEAD)

    def fold_max(s):
        return jnp.max(s.reshape(-1, 8, WIDE), axis=0)

    def fold_sum(s):
        return jnp.sum(s.reshape(-1, 8, WIDE), axis=0)

    def masked(s, half):
        row = lax.broadcasted_iota(jnp.int32, (ROWS, WIDE), 0)
        query = lax.rem(lax.broadcasted_iota(jnp.int32, (ROWS, WIDE), 1), ROWS)
        parts = []
        for tile in range(8):
            tile_y, tile_x = tile // 4, (0, 1, 3, 2)[tile % 4]
            rank = (1 - tile_y if half else tile_y) * 4 + tile_x
            seen = row <= query + (span_tile[half] - rank) * ROWS
            parts.append(jnp.where(seen, s[tile * ROWS : (tile + 1) * ROWS], NEG))
        return jnp.concatenate(parts, axis=0)

    top[...] = jnp.full((2, 8, WIDE), NEG, F32)

    def own_scores(job, half, which, mask):
        s = dot_t(half_of(k_own, half), q_n[which])
        if mask:
            s = masked(s, half)
        s_own[job] = s
        top[which] = jnp.maximum(top[which], fold_max(s))

    def side_scores(keys, scores, pick):
        s = dot_t(half_of(keys, 0), q_n[1])
        scores[0] = s
        top_up = jnp.maximum(top[1], fold_max(s))
        t = dot_t(half_of(keys, pick), q_n[pick])
        scores[1] = t
        peak = fold_max(t)
        top[0] = jnp.maximum(top[0], jnp.where(pick == 0, peak, NEG))
        top[1] = jnp.maximum(top_up, jnp.where(pick == 1, peak, NEG))

    heads_all(0).wait_recv()
    own_scores(0, 0, 1, False)
    for step in STEPS:
        arrive(1, 0, step)
    own_scores(1, 0, 0, True)
    own_scores(2, 1, 1, True)
    for second in STEPS:
        for first in STEPS:
            arrive(1, first, second)
    sib_all(1).start()
    sib_all(0).wait_recv()
    side_scores(k_sib, s_sib, sib_pick)
    far_all(0).wait_recv()
    side_scores(k_far, s_far, far_pick)

    for s in range(2):
        top[s, pl.ds(0, 1)] = jnp.max(top[s], axis=0, keepdims=True) * EXP2_SCALE
    total[...] = jnp.zeros((2, 8, WIDE), F32)
    out_t[...] = jnp.zeros((2, HEAD, WIDE), F32)

    def weigh(scores, weights, job, vals, half, which):
        peak = top[which, pl.ds(0, 1)]
        add = jnp.zeros((8, WIDE), F32)
        for i in range(4):
            rows = pl.ds(256 * i, 256)
            w = jnp.exp2(scores[job, rows] * EXP2_SCALE - peak)
            weights[job, rows] = w.astype(BF16)
            add = add + fold_sum(w)
        return add, dot(half_of(vals, half).T, weights[job])

    def own_weights(job, half, which):
        add, part = weigh(s_own, w_own, job, v_own, half, which)
        total[which] += add
        out_t[which] += part

    def side_weights(vals, scores, weights, pick):
        add, part = weigh(scores, weights, 0, vals, 0, 1)
        add2, part2 = weigh(scores, weights, 1, vals, pick, pick)
        total[0] += jnp.where(pick == 0, add2, 0.0)
        total[1] += add + jnp.where(pick == 1, add2, 0.0)
        out_t[0] += jnp.where(pick == 0, part2, 0.0)
        out_t[1] += part + jnp.where(pick == 1, part2, 0.0)

    own_weights(0, 0, 1)
    own_weights(1, 0, 0)
    own_weights(2, 1, 1)
    sib_all(1).wait_recv()
    side_weights(v_sib, s_sib, w_sib, sib_pick)
    far_all(1).wait_recv()
    side_weights(v_far, s_far, w_far, far_pick)

    o_copy = remote(
        src_ref=o_out, dst_ref=att_ref.at[:, own_cols], send_sem=par_send.at[2],
        recv_sem=par_recv.at[2], device_id=partner,
    )
    dq_copy = remote(
        src_ref=dq_out, dst_ref=gq_ref.at[:, own_cols], send_sem=par_send.at[3],
        recv_sem=par_recv.at[3], device_id=partner,
    )

    def finish(index, dest, base):
        recip = 1.0 / jnp.sum(total[index], axis=0, keepdims=True)
        for head in range(4):
            cols = slice(head * HEAD, (head + 1) * HEAD)
            recip_row = recip[:, cols]
            o = (out_t[index, :, pl.ds(head * HEAD, HEAD)] * recip_row).astype(BF16).T
            dest[:, pl.ds(pl.multiple_of(base + head * HEAD, HEAD), HEAD)] = o
            rows = pl.ds(head * HEAD, HEAD)
            grads = do_n[index, rows, :].astype(F32)
            along = jnp.sum(grads * o.astype(F32), axis=1, keepdims=True)
            along_row = jnp.broadcast_to(along, (ROWS, 8)).T[0:1]
            delta[index, :, pl.ds(head * HEAD, HEAD)] = along_row * recip_row
            recip_col = jnp.broadcast_to(recip_row, (8, ROWS)).T[:, 0:1]
            do_n[index, rows, :] = (grads * recip_col).astype(BF16)

    heads_all(1).wait_recv()
    finish(1 - side, o_out, 0)
    finish(side, att_ref, side * WIDE)

    def grid_slice(full, other=None):
        picks = []
        for axis in range(4):
            if axis in full:
                picks.append(pl.ds(0, 2))
            elif axis == other:
                picks.append(pl.ds(1 - mine[axis], 1))
            else:
                picks.append(pl.ds(mine[axis], 1))
        return tuple(picks)

    def reduce_part(family, quarter, step, send):
        full = [(quarter + t) % 4 for t in range(step + 1, 4)]
        where = grid_slice(full, (quarter + step) % 4 if send else None)
        return (KIND[family],) + where + (pl.ds(32 * quarter, 32),)

    def reduce_copy(family, quarter, step):
        span = pl.ds(OFFSET[step], 8 >> step)
        return remote(
            src_ref=red_out.at[family, quarter, span], dst_ref=red_in.at[family, quarter, span],
            send_sem=red_send.at[family, quarter, step],
            recv_sem=red_recv.at[family, quarter, step],
            device_id=near(across[(quarter + step) % 4]),
        )

    def held(family, where, step):
        part = (acc_own if IS_OWN[family] else acc_far)[where]
        if IS_OWN[family] and step == 0:
            part = part + g_sib_in[where].astype(F32)
        return part

    def reduce_send(family, step):
        for quarter in range(4):
            part = held(family, reduce_part(family, quarter, step, True), step)
            red_out[family, quarter, pl.ds(OFFSET[step], 8 >> step)] = part.reshape(
                8 >> step, 32, HEAD
            ).astype(BF16)
            reduce_copy(family, quarter, step).start()

    def reduce_take(family, step):
        acc = acc_own if IS_OWN[family] else acc_far
        for quarter in range(4):
            reduce_copy(family, quarter, step).wait_recv()
            where = reduce_part(family, quarter, step, False)
            part = held(family, where, step)
            came = red_in[family, quarter, pl.ds(OFFSET[step], 8 >> step)]
            acc[where] = part + came.astype(F32).reshape(part.shape)

    def reduce_next(family, step):
        reduce_take(family, step)
        reduce_send(family, step + 1)

    def far_copy(kind):
        return remote(
            src_ref=far_out.at[kind], dst_ref=far_in.at[kind], send_sem=par_send.at[4 + kind],
            recv_sem=par_recv.at[4 + kind], device_id=farther,
        )

    def far_finish(family):
        reduce_take(family, 3)
        kind = KIND[family]
        far_out[kind] = acc_far[(kind,) + mine].astype(BF16)
        far_copy(kind).start()

    def sib_copy(kind):
        return remote(
            src_ref=g_sib.at[kind], dst_ref=g_sib_in.at[kind],
            send_sem=gs_send.at[kind], recv_sem=gs_recv.at[kind], device_id=sibling,
        )

    def store(ref, kind, half, value):
        ref[kind, half] = value.reshape(2, 2, 2, ROWS, HEAD).astype(ref.dtype)

    def side_dv(weights, pick, ref):
        dv = dot(weights[0], do_n[1])
        dv2 = dot(weights[1], do_n[pick])
        store(ref, 1, 0, dv + jnp.where(pick == 0, dv2, 0.0))
        store(ref, 1, 1, jnp.where(pick == 1, dv2, 0.0))

    def back_dk(vals, half, weights, job, which):
        dp = dot_t(half_of(vals, half), do_n[which])
        ds = (weights[job].astype(F32) * (dp - delta[which])).astype(BF16)
        weights[job] = ds
        return dot(ds, q_n[which]) * SCALE

    def side_dk(vals, weights, pick, ref):
        dk = back_dk(vals, 0, weights, 0, 1)
        dk2 = back_dk(vals, pick, weights, 1, pick)
        store(ref, 0, 0, dk + jnp.where(pick == 0, dk2, 0.0))
        store(ref, 0, 1, jnp.where(pick == 1, dk2, 0.0))

    side_dv(w_far, far_pick, acc_far)
    reduce_send(FAR_V, 0)
    side_dk(v_far, w_far, far_pick, acc_far)
    reduce_send(FAR_K, 0)
    side_dv(w_sib, sib_pick, g_sib)
    sib_copy(1).start()
    o_copy.start()
    side_dk(v_sib, w_sib, sib_pick, g_sib)
    sib_copy(0).start()
    reduce_next(FAR_V, 0)
    store(acc_own, 1, 0, dot(w_own[0], do_n[1]) + dot(w_own[1], do_n[0]))
    store(acc_own, 1, 1, dot(w_own[2], do_n[1]))
    sib_copy(1).wait_recv()
    reduce_send(OWN_V, 0)
    reduce_next(FAR_K, 0)
    store(acc_own, 0, 0, back_dk(v_own, 0, w_own, 0, 1) + back_dk(v_own, 0, w_own, 1, 0))
    store(acc_own, 0, 1, back_dk(v_own, 1, w_own, 2, 1))
    sib_copy(0).wait_recv()
    reduce_send(OWN_K, 0)
    reduce_next(FAR_V, 1)
    reduce_next(FAR_K, 1)

    dq_t[...] = jnp.zeros((2, HEAD, WIDE), F32)

    def back_dq(keys, half, weights, job):
        return dot(half_of(keys, half).T, weights[job])

    def side_dq(keys, weights, pick):
        dq = back_dq(keys, 0, weights, 0)
        dq2 = back_dq(keys, pick, weights, 1)
        dq_t[0] += jnp.where(pick == 0, dq2, 0.0)
        dq_t[1] += dq + jnp.where(pick == 1, dq2, 0.0)

    side_dq(k_far, w_far, far_pick)
    side_dq(k_sib, w_sib, sib_pick)
    reduce_next(OWN_V, 0)
    reduce_next(OWN_K, 0)
    reduce_next(FAR_V, 2)
    reduce_next(FAR_K, 2)
    dq_t[0] += back_dq(k_own, 0, w_own, 1)
    dq_t[1] += back_dq(k_own, 0, w_own, 0) + back_dq(k_own, 1, w_own, 2)

    def finish_dq(index, dest, base):
        grads = (dq_t[index] * SCALE).astype(BF16)
        for head in range(4):
            cols = slice(head * HEAD, (head + 1) * HEAD)
            dest[:, pl.ds(pl.multiple_of(base + head * HEAD, HEAD), HEAD)] = grads[:, cols].T

    reduce_next(OWN_V, 1)
    reduce_next(OWN_K, 1)
    finish_dq(1 - side, dq_out, 0)
    dq_copy.start()
    far_finish(FAR_V)
    far_finish(FAR_K)
    finish_dq(side, gq_ref, side * WIDE)
    reduce_next(OWN_V, 2)
    reduce_next(OWN_K, 2)
    reduce_take(OWN_V, 3)
    reduce_take(OWN_K, 3)
    far_copy(1).wait_recv()
    gv_ref[...] = (acc_own[(1,) + mine] + far_in[1].astype(F32)).astype(BF16)
    far_copy(0).wait_recv()
    gk_ref[...] = (acc_own[(0,) + mine] + far_in[0].astype(F32)).astype(BF16)

    o_copy.wait_recv()
    dq_copy.wait_recv()
    for copy in (heads_all(0), heads_all(1), o_copy, dq_copy):
        copy.wait_send()
    for kind in range(2):
        far_copy(kind).wait_send()
        sib_copy(kind).wait_send()
        sib_all(kind).wait_send()
        far_all(kind).wait_send()
        for first in range(4):
            for second in range(4):
                if first + second:
                    spread(kind, first, second, False).wait_send()
    for family in range(4):
        for step in range(4):
            for quarter in range(4):
                reduce_copy(family, quarter, step).wait_send()


def hand_out(*refs):
    for source, dest in zip(refs[:4], refs[4:]):
        dest[...] = source[...]


def body(queries, key_rows, values, out_grad, span_order):
    vmem = pl.BlockSpec(memory_space=pltpu.VMEM)
    kv = pltpu.VMEM((2, 2, 2, 2, ROWS, HEAD), BF16)
    dma = pltpu.SemaphoreType.DMA
    results = pl.pallas_call(
        kernel,
        out_shape=(
            jax.ShapeDtypeStruct(queries.shape, BF16),
            jax.ShapeDtypeStruct(queries.shape, BF16),
            jax.ShapeDtypeStruct(key_rows.shape, BF16),
            jax.ShapeDtypeStruct(key_rows.shape, BF16),
        ),
        in_specs=[vmem] * 4 + [pl.BlockSpec(memory_space=pltpu.SMEM)],
        out_specs=(vmem,) * 4,
        scratch_shapes=[
            kv, kv, kv, kv, kv, kv,
            pltpu.VMEM((2, WIDE, HEAD), BF16), pltpu.VMEM((2, WIDE, HEAD), BF16),
            pltpu.VMEM((2, 1024, WIDE), F32), pltpu.VMEM((2, 1024, WIDE), F32),
            pltpu.VMEM((3, 1024, WIDE), F32),
            pltpu.VMEM((2, 1024, WIDE), BF16), pltpu.VMEM((2, 1024, WIDE), BF16),
            pltpu.VMEM((3, 1024, WIDE), BF16),
            pltpu.VMEM((2, 8, WIDE), F32), pltpu.VMEM((2, 8, WIDE), F32),
            pltpu.VMEM((2, HEAD, WIDE), F32), pltpu.VMEM((2, HEAD, WIDE), F32),
            pltpu.VMEM((2, 1, WIDE), F32),
            pltpu.VMEM((2, 2, 2, 2, 2, ROWS, HEAD), F32),
            pltpu.VMEM((2, 2, 2, 2, 2, ROWS, HEAD), F32),
            pltpu.VMEM((2, 2, 2, 2, 2, ROWS, HEAD), BF16),
            pltpu.VMEM((2, 2, 2, 2, 2, ROWS, HEAD), BF16),
            pltpu.VMEM((4, 4, 15, 32, HEAD), BF16), pltpu.VMEM((4, 4, 15, 32, HEAD), BF16),
            pltpu.VMEM((2, ROWS, HEAD), BF16), pltpu.VMEM((2, ROWS, HEAD), BF16),
            pltpu.VMEM((ROWS, WIDE), BF16), pltpu.VMEM((ROWS, WIDE), BF16),
            dma((2, 16)), dma((2, 16)), dma((2,)), dma((2,)), dma((2,)), dma((2,)),
            dma((6,)), dma((6,)), dma((2,)), dma((2,)), dma((4, 4, 4)), dma((4, 4, 4)),
        ],
        compiler_params=pltpu.CompilerParams(
            collective_id=0, has_side_effects=True, vmem_limit_bytes=56 * 1024 * 1024
        ),
        cost_estimate=pl.CostEstimate(
            flops=5 * 10**9, bytes_accessed=2 * 10**6, transcendentals=3 * 10**6
        ),
    )(queries, key_rows, values, out_grad, span_order)
    return pl.pallas_call(
        hand_out,
        out_shape=tuple(jax.ShapeDtypeStruct(r.shape, r.dtype) for r in results),
        in_specs=[vmem] * 4,
        out_specs=(vmem,) * 4,
    )(*results)


def solution(mesh):
    rows = P(("grp", "blk"), None)
    return jax.shard_map(
        body,
        mesh=mesh,
        in_specs=(rows, rows, rows, rows, P()),
        out_specs=(rows, rows, rows, rows),
        check_vma=False,
    )
```

```python
import functools
import math

import jax
import jax.numpy as jnp
from jax import lax
from jax.experimental import pallas as pl
from jax.experimental.pallas import tpu as pltpu
from jax.sharding import PartitionSpec as P

HEAD = 128
ROWS = 128
WIDE = 512
NEG = -1e30
SCALE = 1.0 / math.sqrt(HEAD)
EXP2_SCALE = SCALE * math.log2(math.e)
F32 = jnp.float32
BF16 = jnp.bfloat16

STEPS = (1, 3, 2)
FAR_V, OWN_V, FAR_K, OWN_K = range(4)
IS_OWN = (False, True, False, True)
KIND = (1, 1, 0, 0)


def dot(a, b):
    return jnp.dot(a, b, preferred_element_type=F32)


def dot_t(a, b):
    return lax.dot_general(a, b, (((1,), (1,)), ((), ())), preferred_element_type=F32)


def kernel(
    q_ref, k_ref, v_ref, do_ref, order_ref,
    att_ref, gq_ref, gk_ref, gv_ref,
    k_own, v_own, k_far, v_far, k_sib, v_sib,
    q_n, do_n,
    s_far, s_sib, s_own, w_far, w_sib, w_own,
    top, total, out_t, dq_t, delta,
    acc_far, acc_own, g_sib, g_sib_in,
    red_out, red_in, far_out, far_in, o_out, dq_out,
    gat_send, gat_recv, sib_send, sib_recv, far_send, far_recv,
    par_send, par_recv, gs_send, gs_recv, red_send, red_recv,
):
    grp = lax.axis_index("grp")
    blk = lax.axis_index("blk")
    y, x = lax.div(grp, 4), lax.rem(grp, 4)
    core = lax.rem(blk, 2)
    sib_blk = blk + 1 - 2 * core
    far_blk = lax.rem(blk + 15 + 2 * core, 16)
    side = lax.div(grp, 8)
    early_y = jnp.where(y < 2, y, 3 - y)
    span_tile = (early_y * 4 + x, (1 - early_y) * 4 + x)

    def flip(v):
        return v + 1 - 2 * lax.rem(v, 2)

    def near(grp_id):
        return {"grp": grp_id, "blk": blk}

    def shifted(first, second):
        step_x = first + core * (second - first)
        step_y = second + core * (first - second)
        return lax.rem(y + step_y, 4) * 4 + lax.rem(x + step_x, 4)

    across = ((3 - y) * 4 + x, flip(y) * 4 + x, y * 4 + 3 - x, y * 4 + flip(x))
    partner = near(across[0])
    sibling = {"grp": grp, "blk": sib_blk}
    farther = {"grp": grp, "blk": far_blk}

    def place(grp_id):
        py, px = lax.div(grp_id, 4), lax.rem(grp_id, 4)
        return (
            lax.div(py, 2), lax.rem(lax.div(py + 1, 2), 2),
            lax.div(px, 2), lax.rem(lax.div(px + 1, 2), 2),
        )

    mine = place(grp)
    remote = functools.partial(
        pltpu.make_async_remote_copy, device_id_type=pl.DeviceIdType.MESH
    )

    barrier = pltpu.get_barrier_semaphore()
    meet = tuple(near(shifted(s, 0)) for s in STEPS) + tuple(near(shifted(0, s)) for s in STEPS)
    for dev in meet + (sibling, farther):
        pl.semaphore_signal(barrier, inc=1, device_id=dev, device_id_type=pl.DeviceIdType.MESH)

    k_own[mine] = k_ref[...]
    v_own[mine] = v_ref[...]
    own_cols = pl.ds(pl.multiple_of(side * WIDE, WIDE), WIDE)

    def stack(source, dest):
        for head in range(4):
            cols = pl.ds(pl.multiple_of(side * WIDE + head * HEAD, HEAD), HEAD)
            dest[side, pl.ds(head * HEAD, HEAD), :] = source[:, cols]

    pl.semaphore_wait(barrier, 8)

    own_kv, far_kv, sib_kv = (k_own, v_own), (k_far, v_far), (k_sib, v_sib)

    def spread(kind, first, second, arriving):
        along_first = second == 0
        if arriving:
            spot = place(shifted((4 - first) % 4, (4 - second) % 4))
        else:
            spot = mine if along_first else place(shifted((4 - first) % 4, 0))
        return remote(
            src_ref=own_kv[kind].at[spot], dst_ref=own_kv[kind].at[spot],
            send_sem=gat_send.at[kind, first * 4 + second],
            recv_sem=gat_recv.at[kind, first * 4 + second],
            device_id=near(shifted(first, 0) if along_first else shifted(0, second)),
        )

    def hand_far(kind, spot):
        return remote(
            src_ref=own_kv[kind].at[spot], dst_ref=far_kv[kind].at[spot],
            send_sem=far_send.at[kind], recv_sem=far_recv.at[kind], device_id=farther,
        )

    def far_all(kind):
        return remote(
            src_ref=own_kv[kind], dst_ref=far_kv[kind],
            send_sem=far_send.at[kind], recv_sem=far_recv.at[kind], device_id=farther,
        )

    def sib_all(kind):
        return remote(
            src_ref=own_kv[kind], dst_ref=sib_kv[kind],
            send_sem=sib_send.at[kind], recv_sem=sib_recv.at[kind], device_id=sibling,
        )

    def give_head(index, head):
        source, dest = ((q_ref, q_n), (do_ref, do_n))[index]
        cols = pl.ds(pl.multiple_of((1 - side) * WIDE + head * HEAD, HEAD), HEAD)
        return remote(
            src_ref=source.at[:, cols], dst_ref=dest.at[side, pl.ds(head * HEAD, HEAD)],
            send_sem=par_send.at[index], recv_sem=par_recv.at[index], device_id=partner,
        )

    def heads_all(index):
        dest = (q_n, do_n)[index].at[1 - side]
        return remote(
            src_ref=dest, dst_ref=dest,
            send_sem=par_send.at[index], recv_sem=par_recv.at[index], device_id=partner,
        )

    def begin(kind):
        for step in reversed(STEPS):
            spread(kind, step, 0, False).start()
        for step in reversed(STEPS):
            spread(kind, 0, step, False).start()

    def arrive(kind, first, second):
        spread(kind, first, second, True).wait_recv()
        if second == 0:
            for step in reversed(STEPS):
                spread(kind, first, step, False).start()
        hand_far(kind, place(shifted((4 - first) % 4, (4 - second) % 4))).start()

    begin(0)
    hand_far(0, mine).start()
    for head in range(4):
        give_head(0, head).start()
    begin(1)
    stack(q_ref, q_n)
    stack(do_ref, do_n)
    for step in STEPS:
        arrive(0, step, 0)
    for step in STEPS:
        arrive(0, 0, step)
    hand_far(1, mine).start()
    for step in STEPS:
        arrive(1, step, 0)
    for second in STEPS:
        for first in STEPS:
            arrive(0, first, second)
    sib_all(0).start()
    for head in range(4):
        give_head(1, head).start()

    my_rank = order_ref[blk]
    sib_pick = jnp.where(order_ref[sib_blk] < my_rank, 0, 1)
    far_pick = jnp.where(order_ref[far_blk] < my_rank, 0, 1)

    def half_of(ref, half):
        return ref[half].reshape(8 * ROWS, HEAD)

    def fold_max(s):
        return jnp.max(s.reshape(-1, 8, WIDE), axis=0)

    def fold_sum(s):
        return jnp.sum(s.reshape(-1, 8, WIDE), axis=0)

    def masked(s, half):
        row = lax.broadcasted_iota(jnp.int32, (ROWS, WIDE), 0)
        query = lax.rem(lax.broadcasted_iota(jnp.int32, (ROWS, WIDE), 1), ROWS)
        parts = []
        for tile in range(8):
            tile_y, tile_x = tile // 4, (0, 1, 3, 2)[tile % 4]
            rank = (1 - tile_y if half else tile_y) * 4 + tile_x
            seen = row <= query + (span_tile[half] - rank) * ROWS
            parts.append(jnp.where(seen, s[tile * ROWS : (tile + 1) * ROWS], NEG))
        return jnp.concatenate(parts, axis=0)

    top[...] = jnp.full((2, 8, WIDE), NEG, F32)

    def own_scores(job, half, which, mask):
        s = dot_t(half_of(k_own, half), q_n[which])
        if mask:
            s = masked(s, half)
        s_own[job] = s
        top[which] = jnp.maximum(top[which], fold_max(s))

    def side_scores(keys, scores, pick):
        s = dot_t(half_of(keys, 0), q_n[1])
        scores[0] = s
        top_up = jnp.maximum(top[1], fold_max(s))
        t = dot_t(half_of(keys, pick), q_n[pick])
        scores[1] = t
        peak = fold_max(t)
        top[0] = jnp.maximum(top[0], jnp.where(pick == 0, peak, NEG))
        top[1] = jnp.maximum(top_up, jnp.where(pick == 1, peak, NEG))

    heads_all(0).wait_recv()
    own_scores(0, 0, 1, False)
    for step in STEPS:
        arrive(1, 0, step)
    own_scores(1, 0, 0, True)
    own_scores(2, 1, 1, True)
    for second in STEPS:
        for first in STEPS:
            arrive(1, first, second)
    sib_all(1).start()
    sib_all(0).wait_recv()
    side_scores(k_sib, s_sib, sib_pick)
    far_all(0).wait_recv()
    side_scores(k_far, s_far, far_pick)

    for s in range(2):
        top[s, pl.ds(0, 1)] = jnp.max(top[s], axis=0, keepdims=True) * EXP2_SCALE
    total[...] = jnp.zeros((2, 8, WIDE), F32)
    out_t[...] = jnp.zeros((2, HEAD, WIDE), F32)

    def weigh(scores, weights, job, vals, half, which):
        peak = top[which, pl.ds(0, 1)]
        add = jnp.zeros((8, WIDE), F32)
        for i in range(4):
            rows = pl.ds(256 * i, 256)
            w = jnp.exp2(scores[job, rows] * EXP2_SCALE - peak)
            weights[job, rows] = w.astype(BF16)
            add = add + fold_sum(w)
        return add, dot(half_of(vals, half).T, weights[job])

    def own_weights(job, half, which):
        add, part = weigh(s_own, w_own, job, v_own, half, which)
        total[which] += add
        out_t[which] += part

    def side_weights(vals, scores, weights, pick):
        add, part = weigh(scores, weights, 0, vals, 0, 1)
        add2, part2 = weigh(scores, weights, 1, vals, pick, pick)
        total[0] += jnp.where(pick == 0, add2, 0.0)
        total[1] += add + jnp.where(pick == 1, add2, 0.0)
        out_t[0] += jnp.where(pick == 0, part2, 0.0)
        out_t[1] += part + jnp.where(pick == 1, part2, 0.0)

    own_weights(0, 0, 1)
    own_weights(1, 0, 0)
    own_weights(2, 1, 1)
    sib_all(1).wait_recv()
    side_weights(v_sib, s_sib, w_sib, sib_pick)
    far_all(1).wait_recv()
    side_weights(v_far, s_far, w_far, far_pick)

    o_copy = remote(
        src_ref=o_out, dst_ref=att_ref.at[:, own_cols], send_sem=par_send.at[2],
        recv_sem=par_recv.at[2], device_id=partner,
    )
    dq_copy = remote(
        src_ref=dq_out, dst_ref=gq_ref.at[:, own_cols], send_sem=par_send.at[3],
        recv_sem=par_recv.at[3], device_id=partner,
    )

    def finish(index, dest, base):
        recip = 1.0 / jnp.sum(total[index], axis=0, keepdims=True)
        for head in range(4):
            cols = slice(head * HEAD, (head + 1) * HEAD)
            recip_row = recip[:, cols]
            o = (out_t[index, :, pl.ds(head * HEAD, HEAD)] * recip_row).astype(BF16).T
            dest[:, pl.ds(pl.multiple_of(base + head * HEAD, HEAD), HEAD)] = o
            rows = pl.ds(head * HEAD, HEAD)
            grads = do_n[index, rows, :].astype(F32)
            along = jnp.sum(grads * o.astype(F32), axis=1, keepdims=True)
            along_row = jnp.broadcast_to(along, (ROWS, 8)).T[0:1]
            delta[index, :, pl.ds(head * HEAD, HEAD)] = along_row * recip_row
            recip_col = jnp.broadcast_to(recip_row, (8, ROWS)).T[:, 0:1]
            do_n[index, rows, :] = (grads * recip_col).astype(BF16)

    heads_all(1).wait_recv()
    finish(1 - side, o_out, 0)
    finish(side, att_ref, side * WIDE)

    def along(first_x, step):
        return lax.rem(x + step, 4) if first_x else lax.rem(y + step, 4)

    def line(v):
        return (pl.ds(lax.div(v, 2), 1), pl.ds(lax.rem(lax.div(v + 1, 2), 2), 1))

    def reduce_part(family, half, phase, step):
        every = (pl.ds(0, 2), pl.ds(0, 2))
        if phase == 0:
            spot = line(along(half == 0, step))
            where = every + spot if half == 0 else spot + every
        else:
            spot = line(along(half == 1, step))
            where = spot + line(x) if half == 0 else line(y) + spot
        return (KIND[family],) + where + (pl.ds(64 * half, 64),)

    def slot(phase, step):
        return pl.ds(4 * (step - 1), 4) if phase == 0 else pl.ds(11 + step, 1)

    def reduce_copy(family, half, phase, step):
        target = along((half == 0) == (phase == 0), step)
        index = 3 * phase + step - 1
        return remote(
            src_ref=red_out.at[family, half, slot(phase, step)],
            dst_ref=red_in.at[family, half, slot(phase, step)],
            send_sem=red_send.at[family, half, index], recv_sem=red_recv.at[family, half, index],
            device_id=near(y * 4 + target if (half == 0) == (phase == 0) else target * 4 + x),
        )

    def held(family, where, phase):
        part = (acc_own if IS_OWN[family] else acc_far)[where]
        if IS_OWN[family] and phase == 0:
            part = part + g_sib_in[where].astype(F32)
        return part

    def reduce_send(family, phase):
        for step in (2, 1, 3):
            for half in range(2):
                part = held(family, reduce_part(family, half, phase, step), phase)
                red_out[family, half, slot(phase, step)] = part.reshape(-1, 64, HEAD).astype(BF16)
                reduce_copy(family, half, phase, step).start()

    def reduce_take(family, phase):
        acc = acc_own if IS_OWN[family] else acc_far
        for half in range(2):
            where = reduce_part(family, half, phase, 0)
            part = held(family, where, phase)
            for step in (1, 3, 2):
                reduce_copy(family, half, phase, step).wait_recv()
                came = red_in[family, half, slot(phase, step)]
                part = part + came.astype(F32).reshape(part.shape)
            acc[where] = part

    def reduce_next(family):
        reduce_take(family, 0)
        reduce_send(family, 1)

    def far_copy(kind):
        return remote(
            src_ref=far_out.at[kind], dst_ref=far_in.at[kind], send_sem=par_send.at[4 + kind],
            recv_sem=par_recv.at[4 + kind], device_id=farther,
        )

    def far_finish(family):
        reduce_take(family, 1)
        kind = KIND[family]
        far_out[kind] = acc_far[(kind,) + mine].astype(BF16)
        far_copy(kind).start()

    def sib_copy(kind):
        return remote(
            src_ref=g_sib.at[kind], dst_ref=g_sib_in.at[kind],
            send_sem=gs_send.at[kind], recv_sem=gs_recv.at[kind], device_id=sibling,
        )

    def store(ref, kind, half, value):
        ref[kind, half] = value.reshape(2, 2, 2, ROWS, HEAD).astype(ref.dtype)

    def side_dv(weights, pick, ref):
        dv = dot(weights[0], do_n[1])
        dv2 = dot(weights[1], do_n[pick])
        store(ref, 1, 0, dv + jnp.where(pick == 0, dv2, 0.0))
        store(ref, 1, 1, jnp.where(pick == 1, dv2, 0.0))

    def back_dk(vals, half, weights, job, which):
        dp = dot_t(half_of(vals, half), do_n[which])
        ds = (weights[job].astype(F32) * (dp - delta[which])).astype(BF16)
        weights[job] = ds
        return dot(ds, q_n[which]) * SCALE

    def side_dk(vals, weights, pick, ref):
        dk = back_dk(vals, 0, weights, 0, 1)
        dk2 = back_dk(vals, pick, weights, 1, pick)
        store(ref, 0, 0, dk + jnp.where(pick == 0, dk2, 0.0))
        store(ref, 0, 1, jnp.where(pick == 1, dk2, 0.0))

    side_dv(w_far, far_pick, acc_far)
    reduce_send(FAR_V, 0)
    side_dk(v_far, w_far, far_pick, acc_far)
    reduce_send(FAR_K, 0)
    side_dv(w_sib, sib_pick, g_sib)
    sib_copy(1).start()
    o_copy.start()
    side_dk(v_sib, w_sib, sib_pick, g_sib)
    sib_copy(0).start()
    reduce_next(FAR_V)
    store(acc_own, 1, 0, dot(w_own[0], do_n[1]) + dot(w_own[1], do_n[0]))
    store(acc_own, 1, 1, dot(w_own[2], do_n[1]))
    sib_copy(1).wait_recv()
    reduce_send(OWN_V, 0)
    store(acc_own, 0, 0, back_dk(v_own, 0, w_own, 0, 1) + back_dk(v_own, 0, w_own, 1, 0))
    store(acc_own, 0, 1, back_dk(v_own, 1, w_own, 2, 1))
    sib_copy(0).wait_recv()
    reduce_send(OWN_K, 0)
    reduce_next(FAR_K)

    dq_t[...] = jnp.zeros((2, HEAD, WIDE), F32)

    def back_dq(keys, half, weights, job):
        return dot(half_of(keys, half).T, weights[job])

    def side_dq(keys, weights, pick):
        dq = back_dq(keys, 0, weights, 0)
        dq2 = back_dq(keys, pick, weights, 1)
        dq_t[0] += jnp.where(pick == 0, dq2, 0.0)
        dq_t[1] += dq + jnp.where(pick == 1, dq2, 0.0)

    side_dq(k_far, w_far, far_pick)
    side_dq(k_sib, w_sib, sib_pick)
    far_finish(FAR_V)
    reduce_next(OWN_V)
    dq_t[0] += back_dq(k_own, 0, w_own, 1)
    dq_t[1] += back_dq(k_own, 0, w_own, 0) + back_dq(k_own, 1, w_own, 2)

    def finish_dq(index, dest, base):
        grads = (dq_t[index] * SCALE).astype(BF16)
        for head in range(4):
            cols = slice(head * HEAD, (head + 1) * HEAD)
            dest[:, pl.ds(pl.multiple_of(base + head * HEAD, HEAD), HEAD)] = grads[:, cols].T

    finish_dq(1 - side, dq_out, 0)
    dq_copy.start()
    far_finish(FAR_K)
    reduce_next(OWN_K)
    finish_dq(side, gq_ref, side * WIDE)
    reduce_take(OWN_V, 1)
    reduce_take(OWN_K, 1)
    far_copy(1).wait_recv()
    gv_ref[...] = (acc_own[(1,) + mine] + far_in[1].astype(F32)).astype(BF16)
    far_copy(0).wait_recv()
    gk_ref[...] = (acc_own[(0,) + mine] + far_in[0].astype(F32)).astype(BF16)

    o_copy.wait_recv()
    dq_copy.wait_recv()
    for copy in (heads_all(0), heads_all(1), o_copy, dq_copy):
        copy.wait_send()
    for kind in range(2):
        far_copy(kind).wait_send()
        sib_copy(kind).wait_send()
        sib_all(kind).wait_send()
        far_all(kind).wait_send()
        for first in range(4):
            for second in range(4):
                if first + second:
                    spread(kind, first, second, False).wait_send()
    for family in range(4):
        for half in range(2):
            for phase in range(2):
                for step in STEPS:
                    reduce_copy(family, half, phase, step).wait_send()


def hand_out(*refs):
    for source, dest in zip(refs[:4], refs[4:]):
        dest[...] = source[...]


def body(queries, key_rows, values, out_grad, span_order):
    vmem = pl.BlockSpec(memory_space=pltpu.VMEM)
    kv = pltpu.VMEM((2, 2, 2, 2, ROWS, HEAD), BF16)
    dma = pltpu.SemaphoreType.DMA
    results = pl.pallas_call(
        kernel,
        out_shape=(
            jax.ShapeDtypeStruct(queries.shape, BF16),
            jax.ShapeDtypeStruct(queries.shape, BF16),
            jax.ShapeDtypeStruct(key_rows.shape, BF16),
            jax.ShapeDtypeStruct(key_rows.shape, BF16),
        ),
        in_specs=[vmem] * 4 + [pl.BlockSpec(memory_space=pltpu.SMEM)],
        out_specs=(vmem,) * 4,
        scratch_shapes=[
            kv, kv, kv, kv, kv, kv,
            pltpu.VMEM((2, WIDE, HEAD), BF16), pltpu.VMEM((2, WIDE, HEAD), BF16),
            pltpu.VMEM((2, 1024, WIDE), F32), pltpu.VMEM((2, 1024, WIDE), F32),
            pltpu.VMEM((3, 1024, WIDE), F32),
            pltpu.VMEM((2, 1024, WIDE), BF16), pltpu.VMEM((2, 1024, WIDE), BF16),
            pltpu.VMEM((3, 1024, WIDE), BF16),
            pltpu.VMEM((2, 8, WIDE), F32), pltpu.VMEM((2, 8, WIDE), F32),
            pltpu.VMEM((2, HEAD, WIDE), F32), pltpu.VMEM((2, HEAD, WIDE), F32),
            pltpu.VMEM((2, 1, WIDE), F32),
            pltpu.VMEM((2, 2, 2, 2, 2, ROWS, HEAD), F32),
            pltpu.VMEM((2, 2, 2, 2, 2, ROWS, HEAD), F32),
            pltpu.VMEM((2, 2, 2, 2, 2, ROWS, HEAD), BF16),
            pltpu.VMEM((2, 2, 2, 2, 2, ROWS, HEAD), BF16),
            pltpu.VMEM((4, 2, 15, 64, HEAD), BF16), pltpu.VMEM((4, 2, 15, 64, HEAD), BF16),
            pltpu.VMEM((2, ROWS, HEAD), BF16), pltpu.VMEM((2, ROWS, HEAD), BF16),
            pltpu.VMEM((ROWS, WIDE), BF16), pltpu.VMEM((ROWS, WIDE), BF16),
            dma((2, 16)), dma((2, 16)), dma((2,)), dma((2,)), dma((2,)), dma((2,)),
            dma((6,)), dma((6,)), dma((2,)), dma((2,)), dma((4, 2, 6)), dma((4, 2, 6)),
        ],
        compiler_params=pltpu.CompilerParams(
            collective_id=0, has_side_effects=True, vmem_limit_bytes=56 * 1024 * 1024
        ),
        cost_estimate=pl.CostEstimate(
            flops=5 * 10**9, bytes_accessed=2 * 10**6, transcendentals=3 * 10**6
        ),
    )(queries, key_rows, values, out_grad, span_order)
    return pl.pallas_call(
        hand_out,
        out_shape=tuple(jax.ShapeDtypeStruct(r.shape, r.dtype) for r in results),
        in_specs=[vmem] * 4,
        out_specs=(vmem,) * 4,
    )(*results)


def solution(mesh):
    rows = P(("grp", "blk"), None)
    return jax.shard_map(
        body,
        mesh=mesh,
        in_specs=(rows, rows, rows, rows, P()),
        out_specs=(rows, rows, rows, rows),
        check_vma=False,
    )
```

```python
import functools
import math

import jax
import jax.numpy as jnp
from jax import lax
from jax.experimental import pallas as pl
from jax.experimental.pallas import tpu as pltpu
from jax.sharding import PartitionSpec as P

HEAD = 128
ROWS = 128
WIDE = 512
NEG = -1e30
SCALE = 1.0 / math.sqrt(HEAD)
EXP2_SCALE = SCALE * math.log2(math.e)
F32 = jnp.float32
BF16 = jnp.bfloat16

STEPS = (1, 3, 2)
FAR_V, OWN_V, FAR_K, OWN_K = range(4)
IS_OWN = (False, True, False, True)
KIND = (1, 1, 0, 0)


def dot(a, b):
    return jnp.dot(a, b, preferred_element_type=F32)


def dot_t(a, b):
    return lax.dot_general(a, b, (((1,), (1,)), ((), ())), preferred_element_type=F32)


def kernel(
    q_ref, k_ref, v_ref, do_ref, order_ref,
    att_ref, gq_ref, gk_ref, gv_ref,
    k_own, v_own, k_far, v_far, k_sib, v_sib,
    q_n, do_n,
    s_far, s_sib, s_own, w_far, w_sib, w_own,
    top, total, out_t, dq_t, delta,
    acc_far, acc_own, g_sib, g_sib_in,
    red_out, red_in, far_out, far_in, o_out, dq_out,
    gat_send, gat_recv, sib_send, sib_recv, far_send, far_recv,
    par_send, par_recv, gs_send, gs_recv, red_send, red_recv,
):
    grp = lax.axis_index("grp")
    blk = lax.axis_index("blk")
    y, x = lax.div(grp, 4), lax.rem(grp, 4)
    core = lax.rem(blk, 2)
    sib_blk = blk + 1 - 2 * core
    far_blk = lax.rem(blk + 15 + 2 * core, 16)
    side = lax.div(grp, 8)
    early_y = jnp.where(y < 2, y, 3 - y)
    span_tile = (early_y * 4 + x, (1 - early_y) * 4 + x)

    def flip(v):
        return v + 1 - 2 * lax.rem(v, 2)

    def near(grp_id):
        return {"grp": grp_id, "blk": blk}

    def shifted(first, second):
        step_x = first + core * (second - first)
        step_y = second + core * (first - second)
        return lax.rem(y + step_y, 4) * 4 + lax.rem(x + step_x, 4)

    across = ((3 - y) * 4 + x, flip(y) * 4 + x, y * 4 + 3 - x, y * 4 + flip(x))
    partner = near(across[0])
    sibling = {"grp": grp, "blk": sib_blk}
    farther = {"grp": grp, "blk": far_blk}

    def place(grp_id):
        py, px = lax.div(grp_id, 4), lax.rem(grp_id, 4)
        return (
            lax.div(py, 2), lax.rem(lax.div(py + 1, 2), 2),
            lax.div(px, 2), lax.rem(lax.div(px + 1, 2), 2),
        )

    mine = place(grp)
    remote = functools.partial(
        pltpu.make_async_remote_copy, device_id_type=pl.DeviceIdType.MESH
    )

    barrier = pltpu.get_barrier_semaphore()
    meet = tuple(near(shifted(s, 0)) for s in STEPS) + tuple(near(shifted(0, s)) for s in STEPS)
    for dev in meet + (sibling, farther):
        pl.semaphore_signal(barrier, inc=1, device_id=dev, device_id_type=pl.DeviceIdType.MESH)

    k_own[mine] = k_ref[...]
    v_own[mine] = v_ref[...]
    own_cols = pl.ds(pl.multiple_of(side * WIDE, WIDE), WIDE)

    def stack(source, dest):
        for head in range(4):
            cols = pl.ds(pl.multiple_of(side * WIDE + head * HEAD, HEAD), HEAD)
            dest[side, pl.ds(head * HEAD, HEAD), :] = source[:, cols]

    pl.semaphore_wait(barrier, 8)

    own_kv, far_kv, sib_kv = (k_own, v_own), (k_far, v_far), (k_sib, v_sib)

    def spread(kind, first, second, arriving):
        along_first = second == 0
        if arriving:
            spot = place(shifted((4 - first) % 4, (4 - second) % 4))
        else:
            spot = mine if along_first else place(shifted((4 - first) % 4, 0))
        return remote(
            src_ref=own_kv[kind].at[spot], dst_ref=own_kv[kind].at[spot],
            send_sem=gat_send.at[kind, first * 4 + second],
            recv_sem=gat_recv.at[kind, first * 4 + second],
            device_id=near(shifted(first, 0) if along_first else shifted(0, second)),
        )

    def hand_far(kind, spot):
        return remote(
            src_ref=own_kv[kind].at[spot], dst_ref=far_kv[kind].at[spot],
            send_sem=far_send.at[kind], recv_sem=far_recv.at[kind], device_id=farther,
        )

    def far_all(kind):
        return remote(
            src_ref=own_kv[kind], dst_ref=far_kv[kind],
            send_sem=far_send.at[kind], recv_sem=far_recv.at[kind], device_id=farther,
        )

    def sib_all(kind):
        return remote(
            src_ref=own_kv[kind], dst_ref=sib_kv[kind],
            send_sem=sib_send.at[kind], recv_sem=sib_recv.at[kind], device_id=sibling,
        )

    def give_head(index, head):
        source, dest = ((q_ref, q_n), (do_ref, do_n))[index]
        cols = pl.ds(pl.multiple_of((1 - side) * WIDE + head * HEAD, HEAD), HEAD)
        return remote(
            src_ref=source.at[:, cols], dst_ref=dest.at[side, pl.ds(head * HEAD, HEAD)],
            send_sem=par_send.at[index], recv_sem=par_recv.at[index], device_id=partner,
        )

    def heads_all(index):
        dest = (q_n, do_n)[index].at[1 - side]
        return remote(
            src_ref=dest, dst_ref=dest,
            send_sem=par_send.at[index], recv_sem=par_recv.at[index], device_id=partner,
        )

    def begin(kind):
        for step in reversed(STEPS):
            spread(kind, step, 0, False).start()
        for step in reversed(STEPS):
            spread(kind, 0, step, False).start()

    def arrive(kind, first, second):
        spread(kind, first, second, True).wait_recv()
        if second == 0:
            for step in reversed(STEPS):
                spread(kind, first, step, False).start()
        hand_far(kind, place(shifted((4 - first) % 4, (4 - second) % 4))).start()

    begin(0)
    hand_far(0, mine).start()
    for head in range(4):
        give_head(0, head).start()
    begin(1)
    stack(q_ref, q_n)
    stack(do_ref, do_n)
    for step in STEPS:
        arrive(0, step, 0)
    for step in STEPS:
        arrive(0, 0, step)
    hand_far(1, mine).start()
    for step in STEPS:
        arrive(1, step, 0)
    for second in STEPS:
        for first in STEPS:
            arrive(0, first, second)
    sib_all(0).start()
    for head in range(4):
        give_head(1, head).start()

    my_rank = order_ref[blk]
    sib_pick = jnp.where(order_ref[sib_blk] < my_rank, 0, 1)
    far_pick = jnp.where(order_ref[far_blk] < my_rank, 0, 1)

    def half_of(ref, half):
        return ref[half].reshape(8 * ROWS, HEAD)

    def fold_max(s):
        return jnp.max(s.reshape(-1, 8, WIDE), axis=0)

    def fold_sum(s):
        return jnp.sum(s.reshape(-1, 8, WIDE), axis=0)

    def masked(s, half):
        row = lax.broadcasted_iota(jnp.int32, (ROWS, WIDE), 0)
        query = lax.rem(lax.broadcasted_iota(jnp.int32, (ROWS, WIDE), 1), ROWS)
        parts = []
        for tile in range(8):
            tile_y, tile_x = tile // 4, (0, 1, 3, 2)[tile % 4]
            rank = (1 - tile_y if half else tile_y) * 4 + tile_x
            seen = row <= query + (span_tile[half] - rank) * ROWS
            parts.append(jnp.where(seen, s[tile * ROWS : (tile + 1) * ROWS], NEG))
        return jnp.concatenate(parts, axis=0)

    top[...] = jnp.full((2, 8, WIDE), NEG, F32)

    def own_scores(job, half, which, mask):
        s = dot_t(half_of(k_own, half), q_n[which])
        if mask:
            s = masked(s, half)
        s_own[job] = s
        top[which] = jnp.maximum(top[which], fold_max(s))

    def side_scores(keys, scores, pick):
        s = dot_t(half_of(keys, 0), q_n[1])
        scores[0] = s
        top_up = jnp.maximum(top[1], fold_max(s))
        t = dot_t(half_of(keys, pick), q_n[pick])
        scores[1] = t
        peak = fold_max(t)
        top[0] = jnp.maximum(top[0], jnp.where(pick == 0, peak, NEG))
        top[1] = jnp.maximum(top_up, jnp.where(pick == 1, peak, NEG))

    heads_all(0).wait_recv()
    own_scores(0, 0, 1, False)
    for step in STEPS:
        arrive(1, 0, step)
    own_scores(1, 0, 0, True)
    own_scores(2, 1, 1, True)
    for second in STEPS:
        for first in STEPS:
            arrive(1, first, second)
    sib_all(1).start()
    sib_all(0).wait_recv()
    side_scores(k_sib, s_sib, sib_pick)
    far_all(0).wait_recv()
    side_scores(k_far, s_far, far_pick)

    for s in range(2):
        top[s, pl.ds(0, 1)] = jnp.max(top[s], axis=0, keepdims=True) * EXP2_SCALE
    total[...] = jnp.zeros((2, 8, WIDE), F32)
    out_t[...] = jnp.zeros((2, HEAD, WIDE), F32)

    def weigh(scores, weights, job, vals, half, which):
        peak = top[which, pl.ds(0, 1)]
        add = jnp.zeros((8, WIDE), F32)
        for i in range(4):
            rows = pl.ds(256 * i, 256)
            w = jnp.exp2(scores[job, rows] * EXP2_SCALE - peak)
            weights[job, rows] = w.astype(BF16)
            add = add + fold_sum(w)
        return add, dot(half_of(vals, half).T, weights[job])

    def own_weights(job, half, which):
        add, part = weigh(s_own, w_own, job, v_own, half, which)
        total[which] += add
        out_t[which] += part

    def side_weights(vals, scores, weights, pick):
        add, part = weigh(scores, weights, 0, vals, 0, 1)
        add2, part2 = weigh(scores, weights, 1, vals, pick, pick)
        total[0] += jnp.where(pick == 0, add2, 0.0)
        total[1] += add + jnp.where(pick == 1, add2, 0.0)
        out_t[0] += jnp.where(pick == 0, part2, 0.0)
        out_t[1] += part + jnp.where(pick == 1, part2, 0.0)

    own_weights(0, 0, 1)
    own_weights(1, 0, 0)
    own_weights(2, 1, 1)
    sib_all(1).wait_recv()
    side_weights(v_sib, s_sib, w_sib, sib_pick)
    far_all(1).wait_recv()
    side_weights(v_far, s_far, w_far, far_pick)

    o_copy = remote(
        src_ref=o_out, dst_ref=att_ref.at[:, own_cols], send_sem=par_send.at[2],
        recv_sem=par_recv.at[2], device_id=partner,
    )
    dq_copy = remote(
        src_ref=dq_out, dst_ref=gq_ref.at[:, own_cols], send_sem=par_send.at[3],
        recv_sem=par_recv.at[3], device_id=partner,
    )

    def finish(index, dest, base):
        recip = 1.0 / jnp.sum(total[index], axis=0, keepdims=True)
        for head in range(4):
            cols = slice(head * HEAD, (head + 1) * HEAD)
            recip_row = recip[:, cols]
            o = (out_t[index, :, pl.ds(head * HEAD, HEAD)] * recip_row).astype(BF16).T
            dest[:, pl.ds(pl.multiple_of(base + head * HEAD, HEAD), HEAD)] = o
            rows = pl.ds(head * HEAD, HEAD)
            grads = do_n[index, rows, :].astype(F32)
            along = jnp.sum(grads * o.astype(F32), axis=1, keepdims=True)
            along_row = jnp.broadcast_to(along, (ROWS, 8)).T[0:1]
            delta[index, :, pl.ds(head * HEAD, HEAD)] = along_row * recip_row
            recip_col = jnp.broadcast_to(recip_row, (8, ROWS)).T[:, 0:1]
            do_n[index, rows, :] = (grads * recip_col).astype(BF16)

    heads_all(1).wait_recv()
    finish(1 - side, o_out, 0)
    finish(side, att_ref, side * WIDE)

    def along(first_x, step):
        return lax.rem(x + step, 4) if first_x else lax.rem(y + step, 4)

    def line(v):
        return (pl.ds(lax.div(v, 2), 1), pl.ds(lax.rem(lax.div(v + 1, 2), 2), 1))

    def reduce_part(family, half, phase, step):
        every = (pl.ds(0, 2), pl.ds(0, 2))
        if phase == 0:
            spot = line(along(half == 0, step))
            where = every + spot if half == 0 else spot + every
        else:
            spot = line(along(half == 1, step))
            where = spot + line(x) if half == 0 else line(y) + spot
        return (KIND[family],) + where + (pl.ds(64 * half, 64),)

    def slot(phase, step):
        return pl.ds(4 * (step - 1), 4) if phase == 0 else pl.ds(11 + step, 1)

    def reduce_copy(family, half, phase, step):
        target = along((half == 0) == (phase == 0), step)
        index = 3 * phase + step - 1
        return remote(
            src_ref=red_out.at[family, half, slot(phase, step)],
            dst_ref=red_in.at[family, half, slot(phase, step)],
            send_sem=red_send.at[family, half, index], recv_sem=red_recv.at[family, half, index],
            device_id=near(y * 4 + target if (half == 0) == (phase == 0) else target * 4 + x),
        )

    def held(family, where, phase):
        part = (acc_own if IS_OWN[family] else acc_far)[where]
        if IS_OWN[family] and phase == 0:
            part = part + g_sib_in[where].astype(F32)
        return part

    def reduce_send(family, phase):
        for step in (2, 1, 3):
            for half in range(2):
                part = held(family, reduce_part(family, half, phase, step), phase)
                red_out[family, half, slot(phase, step)] = part.reshape(-1, 64, HEAD).astype(BF16)
                reduce_copy(family, half, phase, step).start()

    def reduce_take(family, phase):
        acc = acc_own if IS_OWN[family] else acc_far
        for half in range(2):
            where = reduce_part(family, half, phase, 0)
            part = held(family, where, phase)
            for step in (1, 3, 2):
                reduce_copy(family, half, phase, step).wait_recv()
                came = red_in[family, half, slot(phase, step)]
                part = part + came.astype(F32).reshape(part.shape)
            acc[where] = part

    def reduce_next(family):
        reduce_take(family, 0)
        reduce_send(family, 1)

    def far_copy(kind):
        return remote(
            src_ref=far_out.at[kind], dst_ref=far_in.at[kind], send_sem=par_send.at[4 + kind],
            recv_sem=par_recv.at[4 + kind], device_id=farther,
        )

    def far_finish(family):
        reduce_take(family, 1)
        kind = KIND[family]
        far_out[kind] = acc_far[(kind,) + mine].astype(BF16)
        far_copy(kind).start()

    def sib_copy(kind):
        return remote(
            src_ref=g_sib.at[kind], dst_ref=g_sib_in.at[kind],
            send_sem=gs_send.at[kind], recv_sem=gs_recv.at[kind], device_id=sibling,
        )

    def store(ref, kind, half, value):
        ref[kind, half] = value.reshape(2, 2, 2, ROWS, HEAD).astype(ref.dtype)

    def side_dv(weights, pick, ref):
        dv = dot(weights[0], do_n[1])
        dv2 = dot(weights[1], do_n[pick])
        store(ref, 1, 0, dv + jnp.where(pick == 0, dv2, 0.0))
        store(ref, 1, 1, jnp.where(pick == 1, dv2, 0.0))

    def back_dk(vals, half, weights, job, which):
        dp = dot_t(half_of(vals, half), do_n[which])
        ds = (weights[job].astype(F32) * (dp - delta[which])).astype(BF16)
        weights[job] = ds
        return dot(ds, q_n[which]) * SCALE

    def side_dk(vals, weights, pick, ref):
        dk = back_dk(vals, 0, weights, 0, 1)
        dk2 = back_dk(vals, pick, weights, 1, pick)
        store(ref, 0, 0, dk + jnp.where(pick == 0, dk2, 0.0))
        store(ref, 0, 1, jnp.where(pick == 1, dk2, 0.0))

    side_dv(w_far, far_pick, acc_far)
    reduce_send(FAR_V, 0)
    side_dk(v_far, w_far, far_pick, acc_far)
    reduce_send(FAR_K, 0)
    side_dv(w_sib, sib_pick, g_sib)
    sib_copy(1).start()
    o_copy.start()
    side_dk(v_sib, w_sib, sib_pick, g_sib)
    sib_copy(0).start()
    reduce_next(FAR_V)
    store(acc_own, 1, 0, dot(w_own[0], do_n[1]) + dot(w_own[1], do_n[0]))
    store(acc_own, 1, 1, dot(w_own[2], do_n[1]))
    sib_copy(1).wait_recv()
    reduce_send(OWN_V, 0)
    store(acc_own, 0, 0, back_dk(v_own, 0, w_own, 0, 1) + back_dk(v_own, 0, w_own, 1, 0))
    store(acc_own, 0, 1, back_dk(v_own, 1, w_own, 2, 1))
    sib_copy(0).wait_recv()
    reduce_send(OWN_K, 0)
    reduce_next(FAR_K)

    dq_t[...] = jnp.zeros((2, HEAD, WIDE), F32)

    def back_dq(keys, half, weights, job):
        return dot(half_of(keys, half).T, weights[job])

    def side_dq(keys, weights, pick):
        dq = back_dq(keys, 0, weights, 0)
        dq2 = back_dq(keys, pick, weights, 1)
        dq_t[0] += jnp.where(pick == 0, dq2, 0.0)
        dq_t[1] += dq + jnp.where(pick == 1, dq2, 0.0)

    side_dq(k_far, w_far, far_pick)
    side_dq(k_sib, w_sib, sib_pick)
    dq_t[0] += back_dq(k_own, 0, w_own, 1)
    dq_t[1] += back_dq(k_own, 0, w_own, 0) + back_dq(k_own, 1, w_own, 2)
    reduce_next(OWN_V)
    far_finish(FAR_V)

    def finish_dq(index, dest, base):
        grads = (dq_t[index] * SCALE).astype(BF16)
        for head in range(4):
            cols = slice(head * HEAD, (head + 1) * HEAD)
            dest[:, pl.ds(pl.multiple_of(base + head * HEAD, HEAD), HEAD)] = grads[:, cols].T

    finish_dq(1 - side, dq_out, 0)
    dq_copy.start()
    far_finish(FAR_K)
    reduce_next(OWN_K)
    finish_dq(side, gq_ref, side * WIDE)
    reduce_take(OWN_V, 1)
    reduce_take(OWN_K, 1)
    far_copy(1).wait_recv()
    gv_ref[...] = (acc_own[(1,) + mine] + far_in[1].astype(F32)).astype(BF16)
    far_copy(0).wait_recv()
    gk_ref[...] = (acc_own[(0,) + mine] + far_in[0].astype(F32)).astype(BF16)

    o_copy.wait_recv()
    dq_copy.wait_recv()
    for copy in (heads_all(0), heads_all(1), o_copy, dq_copy):
        copy.wait_send()
    for kind in range(2):
        far_copy(kind).wait_send()
        sib_copy(kind).wait_send()
        sib_all(kind).wait_send()
        far_all(kind).wait_send()
        for first in range(4):
            for second in range(4):
                if first + second:
                    spread(kind, first, second, False).wait_send()
    for family in range(4):
        for half in range(2):
            for phase in range(2):
                for step in STEPS:
                    reduce_copy(family, half, phase, step).wait_send()


def hand_out(*refs):
    for source, dest in zip(refs[:4], refs[4:]):
        dest[...] = source[...]


def body(queries, key_rows, values, out_grad, span_order):
    vmem = pl.BlockSpec(memory_space=pltpu.VMEM)
    kv = pltpu.VMEM((2, 2, 2, 2, ROWS, HEAD), BF16)
    dma = pltpu.SemaphoreType.DMA
    results = pl.pallas_call(
        kernel,
        out_shape=(
            jax.ShapeDtypeStruct(queries.shape, BF16),
            jax.ShapeDtypeStruct(queries.shape, BF16),
            jax.ShapeDtypeStruct(key_rows.shape, BF16),
            jax.ShapeDtypeStruct(key_rows.shape, BF16),
        ),
        in_specs=[vmem] * 4 + [pl.BlockSpec(memory_space=pltpu.SMEM)],
        out_specs=(vmem,) * 4,
        scratch_shapes=[
            kv, kv, kv, kv, kv, kv,
            pltpu.VMEM((2, WIDE, HEAD), BF16), pltpu.VMEM((2, WIDE, HEAD), BF16),
            pltpu.VMEM((2, 1024, WIDE), F32), pltpu.VMEM((2, 1024, WIDE), F32),
            pltpu.VMEM((3, 1024, WIDE), F32),
            pltpu.VMEM((2, 1024, WIDE), BF16), pltpu.VMEM((2, 1024, WIDE), BF16),
            pltpu.VMEM((3, 1024, WIDE), BF16),
            pltpu.VMEM((2, 8, WIDE), F32), pltpu.VMEM((2, 8, WIDE), F32),
            pltpu.VMEM((2, HEAD, WIDE), F32), pltpu.VMEM((2, HEAD, WIDE), F32),
            pltpu.VMEM((2, 1, WIDE), F32),
            pltpu.VMEM((2, 2, 2, 2, 2, ROWS, HEAD), F32),
            pltpu.VMEM((2, 2, 2, 2, 2, ROWS, HEAD), F32),
            pltpu.VMEM((2, 2, 2, 2, 2, ROWS, HEAD), BF16),
            pltpu.VMEM((2, 2, 2, 2, 2, ROWS, HEAD), BF16),
            pltpu.VMEM((4, 2, 15, 64, HEAD), BF16), pltpu.VMEM((4, 2, 15, 64, HEAD), BF16),
            pltpu.VMEM((2, ROWS, HEAD), BF16), pltpu.VMEM((2, ROWS, HEAD), BF16),
            pltpu.VMEM((ROWS, WIDE), BF16), pltpu.VMEM((ROWS, WIDE), BF16),
            dma((2, 16)), dma((2, 16)), dma((2,)), dma((2,)), dma((2,)), dma((2,)),
            dma((6,)), dma((6,)), dma((2,)), dma((2,)), dma((4, 2, 6)), dma((4, 2, 6)),
        ],
        compiler_params=pltpu.CompilerParams(
            collective_id=0, has_side_effects=True, vmem_limit_bytes=56 * 1024 * 1024
        ),
        cost_estimate=pl.CostEstimate(
            flops=5 * 10**9, bytes_accessed=2 * 10**6, transcendentals=3 * 10**6
        ),
    )(queries, key_rows, values, out_grad, span_order)
    return pl.pallas_call(
        hand_out,
        out_shape=tuple(jax.ShapeDtypeStruct(r.shape, r.dtype) for r in results),
        in_specs=[vmem] * 4,
        out_specs=(vmem,) * 4,
    )(*results)


def solution(mesh):
    rows = P(("grp", "blk"), None)
    return jax.shard_map(
        body,
        mesh=mesh,
        in_specs=(rows, rows, rows, rows, P()),
        out_specs=(rows, rows, rows, rows),
        check_vma=False,
    )
```
